256 devices in a mesh: coarse: 32 (over z, x), fine: 8 (over y, core).
Axes of the slice: x: 4, y: 4, z: 8, core: 2. Of those that a mesh axis runs over, the one named last changes fastest.
Arguments:
- node_feats: bfloat16 [524288, 256], P(('coarse', 'fine')), may hold values from -6 to 6
- grad_out: bfloat16 [524288, 256], P(('coarse', 'fine')), may hold values from -6 to 6
- cluster_ids: int32 [524288], P(('coarse', 'fine')), may hold values from 0 to 65535, as said below
- halo_lists: int32 [8192], P('coarse'), may hold values from 0 to 2047, as said below
- edge_sources: int32 [262144], P('coarse'), may hold values from 0 to 2303, as said below
- w_edge_in: bfloat16 [512, 256], replicated, may hold values from -0.25 to 0.25
- b_edge_in: bfloat16 [256], replicated, may hold values from -4 to 4
- w_edge_out: bfloat16 [256, 256], replicated, may hold values from -0.375 to 0.375
- w_unpool: bfloat16 [256, 256], replicated, may hold values from -0.375 to 0.375
Outputs:
- grad_feats: bfloat16 [524288, 256], P(('coarse', 'fine'))
- grad_w_in: float32 [512, 256], replicated
- grad_b_in: float32 [256], replicated
- grad_w_out: float32 [256, 256], replicated
- grad_unpool: float32 [256, 256], replicated
The draws below stay inside these ranges and needn't reach their ends.
Inputs may be any that keep to these rules, and one draw needn't show every extreme that they name: `cluster_ids`: the fine nodes on the devices of coarse index g lie in cells g*2048 to (g+1)*2048 - 1. `halo_lists`: each owner's block of 256 entries holds distinct indices. `edge_sources`: each owner's block of 8192 entries takes every value of its range at least once.
All inputs are finite; a program needn't handle non-finite values.
Results may differ from the reference program's by a relative error of at most 0.0065.
Values may be sent and summed in bfloat16 or wider, within the bound.
A program may use at most 128 MiB of HBM per device.

```python
import jax
import jax.numpy as jnp
from jax import lax

H = 256
NF_DEV = 2048
K = 4
CD = 2048
HS = 128
CELLS = 65536
NODES = 524288
EDGES = 262144
N_FINE = 8


def draw_cluster_ids(key, part):
    key = jax.random.fold_in(key, 11)
    row_ids = jnp.arange(NODES, dtype=jnp.int32)
    group_rows = NF_DEV * N_FINE
    groups = row_ids // group_rows
    position = row_ids % group_rows
    local_ids = jax.random.randint(key, (NODES,), 0, CD, dtype=jnp.int32)
    local_ids = jnp.where(position == 0, CD - 1, jnp.where(position == 1, 0, local_ids))
    return (groups * CD + local_ids).astype(jnp.int32)


def one_list(sub_key):
    return jax.random.permutation(sub_key, CD)[:2 * HS].astype(jnp.int32)


def draw_halo_lists(key, part):
    key = jax.random.fold_in(key, 23)
    sub_keys = jax.random.split(key, CELLS // CD)
    return jax.vmap(one_list)(sub_keys).reshape(-1).astype(jnp.int32)


def owner_sources(sub_key):
    first_key, second_key, third_key = jax.random.split(sub_key, 3)
    rows = CD + 2 * HS
    covered = jax.random.permutation(first_key, rows).astype(jnp.int32)
    others = jax.random.randint(second_key, (CD * K - rows,), 0, rows, dtype=jnp.int32)
    joined = jnp.concatenate([covered, others])
    order = jax.random.permutation(third_key, CD * K)
    return jnp.take(joined, order).astype(jnp.int32)


def draw_edge_sources(key, part):
    key = jax.random.fold_in(key, 37)
    sub_keys = jax.random.split(key, CELLS // CD)
    return jax.vmap(owner_sources)(sub_keys).reshape(-1).astype(jnp.int32)


def shard_levels(key, shape, pieces, least, largest):
    factor_of = 1.0
    for axis_at, blocks in pieces:
        steps = jax.random.uniform(jax.random.fold_in(jax.random.fold_in(key, 6), axis_at), (blocks,), jnp.float32, least / len(pieces), largest / len(pieces))
        factor_of = factor_of * jnp.repeat(jnp.exp(steps), shape[axis_at] // blocks).reshape((-1,) + (1,) * (len(shape) - 1 - axis_at))
    return factor_of


def gaussian(stream_key, dims, deviation, bound, shards=(), kind=jnp.bfloat16):
    loudness = shard_levels(stream_key, dims, shards, -0.22, 0.18) if shards else 1.0
    array = jax.random.normal(stream_key, dims, jnp.float32) * deviation * loudness
    return jnp.minimum(jnp.maximum(array, -bound), bound).astype(kind)


def setup_inputs(seed: int = 0) -> dict:
    splits = jax.random.split(jax.random.key(seed), 10)
    return {
        "node_feats": gaussian(splits[0], (NODES, H), 1.0, 6.0, ((0, 256),)),
        "grad_out": gaussian(splits[1], (NODES, H), 1.0, 6.0, ((0, 256),)),
        "cluster_ids": draw_cluster_ids(jax.random.fold_in(splits[9], 71), 0),
        "halo_lists": draw_halo_lists(jax.random.fold_in(splits[9], 71), 0),
        "edge_sources": draw_edge_sources(jax.random.fold_in(splits[9], 71), 0),
        "w_edge_in": gaussian(splits[5], (2 * H, H), (2 * H) ** -0.5, 0.25),
        "b_edge_in": gaussian(splits[6], (H,), 1.0, 4.0),
        "w_edge_out": gaussian(splits[7], (H, H), H ** -0.5, 0.375),
        "w_unpool": gaussian(splits[8], (H, H), H ** -0.5, 0.375),
    }


def edge_work(dst_bf, dst_full, extended, sources, grad_sum_bf, w_edge_in, b_edge_in, w_edge_out, w_unpool):
    row_count = dst_bf.shape[0]
    feature_width = dst_bf.shape[1]
    fan_count = sources.shape[0] // row_count
    dst_rep = jnp.repeat(dst_bf, fan_count, axis=0)
    src_feats = jnp.take(extended, sources, axis=0)
    joined = jnp.concatenate([dst_rep, src_feats], axis=1)
    pre_act = jnp.dot(joined, w_edge_in, preferred_element_type=jnp.float32) + b_edge_in.astype(jnp.float32)
    sigmoid_act = jax.nn.sigmoid(pre_act)
    hidden = (pre_act * sigmoid_act).astype(jnp.bfloat16)
    messages = jnp.dot(hidden, w_edge_out, preferred_element_type=jnp.float32)
    aggregate = messages.reshape(row_count, fan_count, feature_width).sum(axis=1)
    new_coarse = (dst_full + aggregate).astype(jnp.bfloat16)
    grad_new = jnp.dot(grad_sum_bf, w_unpool.T, preferred_element_type=jnp.float32).astype(jnp.bfloat16)
    grad_up = jnp.dot(new_coarse.T, grad_sum_bf, preferred_element_type=jnp.float32)
    grad_msg = jnp.repeat(grad_new, fan_count, axis=0)
    grad_w2 = jnp.dot(hidden.T, grad_msg, preferred_element_type=jnp.float32)
    grad_hidden = jnp.dot(grad_msg, w_edge_out.T, preferred_element_type=jnp.float32)
    grad_act = (grad_hidden * sigmoid_act * (1.0 + pre_act * (1.0 - sigmoid_act))).astype(jnp.bfloat16)
    grad_w1 = jnp.dot(joined.T, grad_act, preferred_element_type=jnp.float32)
    grad_b1 = jnp.sum(grad_act.astype(jnp.float32), axis=0)
    grad_joined = jnp.dot(grad_act, w_edge_in.T, preferred_element_type=jnp.float32)
    grad_dst = grad_new.astype(jnp.float32) + grad_joined[:, :feature_width].reshape(row_count, fan_count, feature_width).sum(axis=1)
    grad_src = jax.ops.segment_sum(grad_joined[:, feature_width:], sources, num_segments=extended.shape[0])
    return grad_dst, grad_src, grad_up, grad_w2, grad_w1, grad_b1


def take_rows(block, indices):
    return jnp.take(block, indices, axis=0)


def scatter_back(for_right, for_left, right_ids, left_ids):
    return jax.ops.segment_sum(for_right, right_ids, num_segments=CD) + jax.ops.segment_sum(for_left, left_ids, num_segments=CD)


def reference(node_feats, grad_out, cluster_ids, halo_lists, edge_sources, w_edge_in, b_edge_in, w_edge_out, w_unpool):
    pooled = jax.ops.segment_sum(node_feats.astype(jnp.float32), cluster_ids, num_segments=CELLS)
    grad_sum = jax.ops.segment_sum(grad_out.astype(jnp.float32), cluster_ids, num_segments=CELLS)
    pooled_bf = pooled.astype(jnp.bfloat16)
    grad_sum_bf = grad_sum.astype(jnp.bfloat16)
    owners = CELLS // CD
    blocks = pooled_bf.reshape(owners, CD, H)
    lists = halo_lists.reshape(owners, 2, HS)
    to_right = jax.vmap(take_rows)(blocks, lists[:, 0])
    to_left = jax.vmap(take_rows)(blocks, lists[:, 1])
    from_left = jnp.roll(to_right, 1, axis=0)
    from_right = jnp.roll(to_left, -1, axis=0)
    extended = jnp.concatenate([blocks, from_left, from_right], axis=1)

    def per_owner(items):
        return edge_work(items[0], items[1], items[2], items[3], items[4], w_edge_in, b_edge_in, w_edge_out, w_unpool)

    grad_dst, grad_src, grad_up, grad_w2, grad_w1, grad_b1 = lax.map(
        per_owner,
        (blocks, pooled.reshape(owners, CD, H), extended, edge_sources.reshape(owners, CD * K), grad_sum_bf.reshape(owners, CD, H)))
    back_left = grad_src[:, CD:CD + HS]
    back_right = grad_src[:, CD + HS:]
    for_right = jnp.roll(back_left, -1, axis=0)
    for_left = jnp.roll(back_right, 1, axis=0)
    returned = jax.vmap(scatter_back)(for_right, for_left, lists[:, 0], lists[:, 1])
    grad_pool = (grad_dst + grad_src[:, :CD] + returned).reshape(CELLS, H)
    grad_feats = (grad_out.astype(jnp.float32) + jnp.take(grad_pool, cluster_ids, axis=0)).astype(jnp.bfloat16)
    edge_scale = float(EDGES) ** -0.5
    cell_scale = float(CELLS) ** -0.5
    return (grad_feats, grad_w1.sum(axis=0) * edge_scale, grad_b1.sum(axis=0) * edge_scale,
            grad_w2.sum(axis=0) * edge_scale, grad_up.sum(axis=0) * cell_scale)
```

```python
import functools

import jax
import jax.numpy as jnp
from jax import lax
from jax.experimental import pallas as pl
from jax.experimental.pallas import tpu as pltpu
from jax.sharding import PartitionSpec as P

MESH = pl.DeviceIdType.MESH
F32 = jnp.float32
BF16 = jnp.bfloat16
I32 = jnp.int32
K = 4
NY = 4
L = 128


def dot(a, b, dims=((1,), (0,))):
    return lax.dot_general(a, b, (dims, ((), ())), preferred_element_type=F32)


def onehot(mask):
    return jnp.where(mask, 1.0, 0.0).astype(BF16)


def columns(row):
    return jnp.transpose(jnp.broadcast_to(row, (L, L)))


class Scatter:
    def __init__(self, place, stage, psend, prcv, ysend, yrcv, sems):
        self.p = place
        self.stage, self.psend, self.prcv = stage, psend, prcv
        self.ysend, self.yrcv = ysend, yrcv
        self.ps, self.pr, self.ys, self.yr = sems
        self.cells = psend.shape[1]
        self.half = self.cells // 2

    def pair(self, r):
        return pltpu.make_async_remote_copy(
            src_ref=self.psend.at[r], dst_ref=self.prcv.at[r],
            send_sem=self.ps.at[r], recv_sem=self.pr.at[r],
            device_id={"fine": self.p["partner"]}, device_id_type=MESH)

    def ring(self, i):
        to = self.p["up"] if i in (0, 2, 4) else self.p["down"]
        return pltpu.make_async_remote_copy(
            src_ref=self.ysend.at[i], dst_ref=self.yrcv.at[i],
            send_sem=self.ys.at[i], recv_sem=self.yr.at[i],
            device_id={"fine": to}, device_id_type=MESH)

    def emit_pair(self, r):
        at = pl.multiple_of((1 - self.p["core"]) * self.cells, self.cells)
        self.psend[r] = self.stage[r, pl.ds(at, self.cells), :].astype(BF16)
        self.pair(r).start()

    def half_sum(self, r, h):
        at = pl.multiple_of(self.p["core"] * self.cells + h * self.half, self.half)
        mine = self.stage[r, pl.ds(at, self.half), :]
        return mine + self.prcv[r, h * self.half:(h + 1) * self.half, :].astype(F32)

    def send(self, i, value):
        self.ysend[i] = value.astype(BF16)
        self.ring(i).start()

    def far(self):
        self.pair(2).wait_recv()
        self.send(0, self.half_sum(2, 0))
        self.send(1, self.half_sum(2, 1))

    def near_up(self):
        self.pair(1).wait_recv()
        self.send(2, self.half_sum(1, 1))

    def near_down(self):
        self.pair(3).wait_recv()
        self.send(3, self.half_sum(3, 0))

    def relay(self):
        self.ring(0).wait_recv()
        self.send(4, self.half_sum(1, 0) + self.yrcv[0].astype(F32))
        self.ring(1).wait_recv()
        self.send(5, self.half_sum(3, 1) + self.yrcv[1].astype(F32))

    def finish(self):
        self.pair(0).wait_recv()
        for i in (2, 3, 4, 5):
            self.ring(i).wait_recv()
        low = self.half_sum(0, 0) + self.yrcv[4].astype(F32) + self.yrcv[3].astype(F32)
        high = self.half_sum(0, 1) + self.yrcv[2].astype(F32) + self.yrcv[5].astype(F32)
        return low, high

    def drain(self):
        for r in range(NY):
            self.pair(r).wait_send()
        for i in range(6):
            self.ring(i).wait_send()


class Gather:
    def __init__(self, place, table, cells, sems):
        self.p, self.table, self.cells = place, table, cells
        self.half = cells // 2
        self.ss, self.rs = sems

    def copy(self, i, to, y, core, h0, rows):
        at = pl.multiple_of((y * 2 + core) * self.cells + h0, self.half)
        ref = self.table.at[pl.ds(at, rows), :]
        return pltpu.make_async_remote_copy(
            src_ref=ref, dst_ref=ref, send_sem=self.ss.at[i], recv_sem=self.rs.at[i],
            device_id={"fine": to}, device_id_type=MESH)

    def out(self, i):
        p, c, h = self.p, self.p["core"], self.half
        y, yu, yd, yf = p["y"], p["y_up"], p["y_down"], p["y_far"]
        return {
            0: lambda: self.copy(0, p["up"], y, c, 0, h),
            1: lambda: self.copy(1, p["down"], y, c, h, h),
            2: lambda: self.copy(2, p["up"], y, c, h, h),
            3: lambda: self.copy(3, p["down"], y, c, 0, h),
            4: lambda: self.copy(4, p["partner"], y, c, 0, 2 * h),
            5: lambda: self.copy(5, p["up"], yd, c, 0, h),
            6: lambda: self.copy(6, p["down"], yu, c, h, h),
            7: lambda: self.copy(7, p["partner"], yd, c, 0, 2 * h),
            8: lambda: self.copy(8, p["partner"], yu, c, 0, 2 * h),
            9: lambda: self.copy(9, p["partner"], yf, c, 0, 2 * h),
        }[i]()

    def arrival(self, i):
        p, c, h = self.p, self.p["core"], self.half
        y, yu, yd, yf = p["y"], p["y_up"], p["y_down"], p["y_far"]
        o = 1 - c
        spec = {
            0: (yd, c, 0, h), 1: (yu, c, h, h), 2: (yd, c, h, h), 3: (yu, c, 0, h),
            4: (y, o, 0, 2 * h), 5: (yf, c, 0, h), 6: (yf, c, h, h),
            7: (yd, o, 0, 2 * h), 8: (yu, o, 0, 2 * h), 9: (yf, o, 0, 2 * h),
        }[i]
        return self.copy(i, p["partner"], *spec)

    def start(self):
        for i in range(5):
            self.out(i).start()

    def relay(self):
        self.arrival(0).wait_recv()
        self.out(5).start()
        self.arrival(1).wait_recv()
        self.out(6).start()

    def share_near(self):
        self.arrival(2).wait_recv()
        self.out(7).start()
        self.arrival(3).wait_recv()
        self.out(8).start()

    def share_far(self):
        self.arrival(5).wait_recv()
        self.arrival(6).wait_recv()
        self.out(9).start()

    def wait(self, *which):
        for i in which:
            self.arrival(i).wait_recv()

    def drain(self):
        for i in range(10):
            self.out(i).wait_send()


def kernel(
    n_coarse, edge_scale, cell_scale,
    nf, go, cid, halo, es, w1, b1, w2, w3,
    out_gf, out_w1, out_b1, out_w2, out_w3,
    pool_mat, unpool_mat, src_mat, src_mat_t, halo_mat, halo_mat_t,
    es_col, es_row,
    st0, st1, st2, psend, prcv, ysend, yrcv,
    ext, gp, hsend, gret, back, src_feats, wide, acc,
    w_part, w_pair_s, w_pair_r, w_rs_s, w_rs_r, w_y, w_ag, w_fin,
    ps, pr, ys, yr, ags, agr, hs_s, hs_r, ar_s, ar_r,
):
    cells = gp.shape[0] // 8
    group = 8 * cells
    nodes, feat = nf.shape
    edges = K * cells
    side = halo.shape[1]
    rows = group + 2 * side
    g = lax.axis_index("coarse")
    f = lax.axis_index("fine")
    core = lax.rem(f, 2)
    y = lax.div(f, 2)
    y_up, y_far, y_down = lax.rem(y + 1, NY), lax.rem(y + 2, NY), lax.rem(y + 3, NY)
    place = {
        "core": core, "y": y, "y_up": y_up, "y_far": y_far, "y_down": y_down,
        "partner": f + 1 - 2 * core, "up": y_up * 2 + core,
        "down": y_down * 2 + core, "far": y_far * 2 + core,
    }
    right, left = lax.rem(g + 1, n_coarse), lax.rem(g + n_coarse - 1, n_coarse)

    barrier = pltpu.get_barrier_semaphore()
    for name in ("partner", "up", "down", "far"):
        pl.semaphore_signal(barrier, inc=1, device_id={"fine": place[name]}, device_id_type=MESH)

    @pl.loop(1, n_coarse)
    def _(t):
        pl.semaphore_signal(
            barrier, inc=1, device_id={"coarse": lax.rem(g + t, n_coarse)}, device_id_type=MESH)

    own = pl.multiple_of(f * cells, cells)
    y_of = (y, y_up, y_far, y_down)

    def pair_rows(r):
        return pl.multiple_of(y_of[r] * 2 * cells, 2 * cells)

    def build_pool(r):
        ids = lax.broadcasted_iota(I32, (2 * cells, L), 0) + (g * group + y_of[r] * 2 * cells)

        @pl.loop(0, nodes // L)
        def _(b):
            row = cid[pl.ds(b, 1), :]
            pool_mat[r, :, pl.ds(pl.multiple_of(b * L, L), L)] = onehot(ids == row)

    sc = [
        Scatter(place, st, psend.at[i], prcv.at[i], ysend.at[i], yrcv.at[i],
                (ps.at[i], pr.at[i], ys.at[i], yr.at[i]))
        for i, st in enumerate((st0, st1, st2))
    ]
    ag0 = Gather(place, ext, cells, (ags.at[0], agr.at[0]))
    ag1 = Gather(place, gp, cells, (ags.at[1], agr.at[1]))

    def pool(r, x, stage):
        stage[r] = dot(pool_mat[r], x[...])

    build_pool(2)
    pool(2, nf, st0)
    pl.semaphore_wait(barrier, 4 + n_coarse - 1)
    sc[0].emit_pair(2)
    build_pool(1)
    pool(1, nf, st0)
    sc[0].emit_pair(1)
    sc[0].far()
    build_pool(3)
    pool(3, nf, st0)
    sc[0].emit_pair(3)
    sc[0].near_up()
    build_pool(0)
    pool(0, nf, st0)
    sc[0].emit_pair(0)
    sc[0].near_down()
    sc[0].relay()
    for r in (2, 1, 3, 0):
        pool(r, go, st1)
        sc[1].emit_pair(r)

    low, high = sc[0].finish()
    half = cells // 2
    wide[0:half] = low
    wide[half:cells] = high
    ext[pl.ds(own, cells), :] = wide[0:cells].astype(BF16)
    ag0.start()
    sc[1].far()

    at_es = pl.multiple_of(f * (edges // L), edges // L)

    @pl.loop(0, edges // L)
    def _(b):
        es_col[pl.ds(pl.multiple_of(b * L, L), L), :] = columns(es[pl.ds(at_es + b, 1), :])

    lane = lax.broadcasted_iota(I32, (L, L), 1)
    sub = lax.broadcasted_iota(I32, (L, L), 0)
    for k in range(K):
        for q in range(cells // L):
            at = k * cells + q * L
            col = es_col[pl.ds(k + q * L * K, L, stride=K), :]
            es_row[at // L:at // L + 1, :] = jnp.transpose(col)[0:1, :]

            @pl.loop(0, rows // L)
            def _(j, col=col, at=at):
                src_mat[at:at + L, pl.ds(pl.multiple_of(j * L, L), L)] = onehot(col == lane + j * L)

    ag0.relay()
    sc[1].near_up()
    sc[1].near_down()
    for q in range(2):
        col = columns(halo[q:q + 1, :])

        @pl.loop(0, group // L)
        def _(j, col=col, q=q):
            halo_mat[q * L:(q + 1) * L, pl.ds(pl.multiple_of(j * L, L), L)] = onehot(
                col == lane + j * L)
    ag0.share_near()
    sc[1].relay()

    @pl.loop(0, rows // L)
    def _(j):
        at = pl.multiple_of(j * L, L)
        for b in range(edges // L):
            src_mat_t[pl.ds(at, L), b * L:(b + 1) * L] = onehot(es_row[b:b + 1, :] == sub + j * L)

    @pl.loop(0, group // L)
    def _(j):
        at = pl.multiple_of(j * L, L)
        for q in range(2):
            halo_mat_t[pl.ds(at, L), q * L:(q + 1) * L] = onehot(halo[q:q + 1, :] == sub + j * L)

    ag0.share_far()

    low, high = sc[1].finish()
    wide[cells:cells + half] = low
    wide[cells + half:2 * cells] = high
    ag0.wait(4, 7, 8, 9)

    def halo_out(q):
        to, row = (right, 0) if q == 0 else (left, side)
        at = group + row
        return pltpu.make_async_remote_copy(
            src_ref=hsend.at[0, q], dst_ref=ext.at[at:at + side, :],
            send_sem=hs_s.at[q], recv_sem=hs_r.at[q],
            device_id={"coarse": to}, device_id_type=MESH)

    picked = dot(halo_mat[...], ext[0:group, :])
    hsend[0, 0] = picked[0:side].astype(BF16)
    hsend[0, 1] = picked[side:2 * side].astype(BF16)
    halo_out(0).start()
    halo_out(1).start()

    gsum = wide[cells:2 * cells].astype(BF16)
    pooled_bf = wide[0:cells].astype(BF16)
    gnew = dot(gsum, w3[...], ((1,), (1,))).astype(BF16)
    ghid = dot(gnew, w2[...], ((1,), (1,)))
    acc[0:edges, :] = dot(src_mat[:, 0:group], ext[0:group, :])
    pre_dst = dot(pooled_bf, w1[0:feat, :]) + b1[...].astype(F32)
    halo_out(0).wait_recv()
    halo_out(1).wait_recv()
    src_feats[...] = (
        acc[0:edges, :] + dot(src_mat[:, group:rows], ext[group:rows, :])
    ).astype(BF16)

    hsum = jnp.zeros((cells, feat), F32)
    gsum_act = jnp.zeros((cells, feat), F32)
    for k in range(K):
        span = slice(k * cells, (k + 1) * cells)
        pre = pre_dst + dot(src_feats[span, :], w1[feat:2 * feat, :])
        sig = 1.0 / (1.0 + jnp.exp(-pre))
        hsum = hsum + (pre * sig).astype(BF16).astype(F32)
        act = (ghid * sig * (1.0 + pre * (1.0 - sig))).astype(BF16)
        gret[span, :] = act
        gsum_act = gsum_act + act.astype(F32)

    def halo_back(q):
        to = left if q == 0 else right
        return pltpu.make_async_remote_copy(
            src_ref=hsend.at[1, q], dst_ref=back.at[pl.ds(q * side, side), :],
            send_sem=hs_s.at[2 + q], recv_sem=hs_r.at[2 + q],
            device_id={"coarse": to}, device_id_type=MESH)

    outer = dot(src_mat_t[group:rows, :], gret[...])
    hsend[1, 0] = outer[0:side].astype(BF16)
    hsend[1, 1] = outer[side:2 * side].astype(BF16)
    halo_back(0).start()
    halo_back(1).start()

    act_bf = gsum_act.astype(BF16)
    hsum_bf = hsum.astype(BF16)
    new_coarse = (wide[0:cells] + dot(hsum_bf, w2[...])).astype(BF16)
    first = ((0,), (0,))
    w_part[0, 0:feat, 0:feat] = dot(pooled_bf, act_bf, first)
    w_part[0, feat:2 * feat, 0:feat] = dot(src_feats[...], gret[...], first)
    w_part[1, 0:feat, 0:feat] = dot(hsum_bf, gnew, first)
    w_part[1, feat:2 * feat, 0:feat] = dot(new_coarse, gsum, first)
    w_part[:, :, feat:] = jnp.zeros((2, 2 * feat, L), F32)
    bias = jnp.sum(gsum_act, axis=0, keepdims=True)
    for q in range(feat // L):
        w_part[0, q * 16:q * 16 + 1, feat:] = bias[:, q * L:(q + 1) * L]

    pair_w = pltpu.make_async_remote_copy(
        src_ref=w_pair_s, dst_ref=w_pair_r, send_sem=ar_s.at[0], recv_sem=ar_r.at[0],
        device_id={"fine": place["partner"]}, device_id_type=MESH)
    w_pair_s[...] = w_part[1 - core].astype(BF16)
    pair_w.start()

    def spread(r):
        at = pair_rows(r)
        return dot(src_mat_t[pl.ds(at, 2 * cells), :], gret[...])

    for r in (2, 1, 3, 0):
        st2[r] = spread(r)
    halo_back(0).wait_recv()
    halo_back(1).wait_recv()

    def add_back(r):
        at = pair_rows(r)
        st2[r] = st2[r] + dot(halo_mat_t[pl.ds(at, 2 * cells), :], back[...])
        sc[2].emit_pair(r)

    add_back(2)
    add_back(1)
    add_back(3)
    sc[2].far()
    add_back(0)
    sc[2].near_up()
    sc[2].near_down()

    piece = w_rs_s.shape[0] // n_coarse
    pair_w.wait_recv()
    w_rs_s[...] = (w_part[core] + w_pair_r[...].astype(F32)).astype(BF16)

    def piece_out(t):
        j = lax.rem(g + t, n_coarse)
        return pltpu.make_async_remote_copy(
            src_ref=w_rs_s.at[pl.ds(pl.multiple_of(j * piece, piece), piece), :],
            dst_ref=w_rs_r.at[pl.ds(pl.multiple_of((n_coarse - 1 - t) * piece, piece), piece), :],
            send_sem=ar_s.at[1], recv_sem=ar_r.at[1],
            device_id={"coarse": j}, device_id_type=MESH)

    @pl.loop(1, n_coarse)
    def _(t):
        piece_out(t).start()

    sc[2].relay()

    @pl.loop(0, nodes // L)
    def _(b):
        col = columns(cid[pl.ds(b, 1), :])
        at = pl.multiple_of(b * L, L)
        for j in range(group // L):
            unpool_mat[pl.ds(at, L), j * L:(j + 1) * L] = onehot(
                col == lane + (g * group + j * L))

    many = pltpu.make_async_remote_copy(
        src_ref=w_rs_r, dst_ref=w_rs_r, send_sem=ar_s.at[1], recv_sem=ar_r.at[1],
        device_id={"coarse": right}, device_id_type=MESH)
    many.wait_recv()
    my_piece = pl.multiple_of(g * piece, piece)
    total = w_rs_s[pl.ds(my_piece, piece), :].astype(F32)
    for t in range(n_coarse - 1):
        total = total + w_rs_r[t * piece:(t + 1) * piece, :].astype(F32)
    w_y[y] = total.astype(BF16)

    def y_out(t):
        return pltpu.make_async_remote_copy(
            src_ref=w_y.at[y], dst_ref=w_y.at[y], send_sem=ar_s.at[1 + t], recv_sem=ar_r.at[1 + t],
            device_id={"fine": y_of[t] * 2 + core}, device_id_type=MESH)

    def y_in(t):
        src = (y, y_down, y_far, y_up)[t]
        return pltpu.make_async_remote_copy(
            src_ref=w_y.at[src], dst_ref=w_y.at[src], send_sem=ar_s.at[1 + t],
            recv_sem=ar_r.at[1 + t], device_id={"fine": place["up"]}, device_id_type=MESH)

    for t in (1, 2, 3):
        y_out(t).start()

    low, high = sc[2].finish()
    src_grad = jnp.concatenate([low, high], axis=0).astype(BF16)
    last = ((1,), (1,))
    gpool = gnew.astype(F32) + dot(act_bf, w1[0:feat, :], last) + dot(src_grad, w1[feat:, :], last)
    gp[pl.ds(own, cells), :] = gpool.astype(BF16)
    ag1.start()

    for t in (1, 2, 3):
        y_in(t).wait_recv()
    summed = w_y[0].astype(F32)
    for t in range(1, NY):
        summed = summed + w_y[t].astype(F32)
    w_ag[pl.ds(my_piece, piece), :] = summed.astype(BF16)

    def piece_back(t):
        ref = w_ag.at[pl.ds(my_piece, piece), :]
        return pltpu.make_async_remote_copy(
            src_ref=ref, dst_ref=ref, send_sem=ar_s.at[5], recv_sem=ar_r.at[5],
            device_id={"coarse": lax.rem(g + t, n_coarse)}, device_id_type=MESH)

    @pl.loop(1, n_coarse)
    def _(t):
        piece_back(t).start()

    ag1.relay()

    def take(y_at, first_pass):
        at = pl.multiple_of(y_at * 2 * cells, 2 * cells)
        part = dot(unpool_mat[:, pl.ds(at, 2 * cells)], gp[pl.ds(at, 2 * cells), :])
        if first_pass:
            acc[...] = part
        else:
            acc[...] += part

    ag1.wait(4)
    take(y, True)
    ag1.share_near()
    ag1.wait(7)
    take(y_down, False)
    ag1.wait(8)
    take(y_up, False)
    ag1.share_far()

    many_back = pltpu.make_async_remote_copy(
        src_ref=w_rs_r, dst_ref=w_ag.at[0:(n_coarse - 1) * piece, :], send_sem=ar_s.at[5],
        recv_sem=ar_r.at[5], device_id={"coarse": right}, device_id_type=MESH)
    many_back.wait_recv()
    w_fin[core] = w_ag[...]
    pair_fin = pltpu.make_async_remote_copy(
        src_ref=w_ag, dst_ref=w_fin.at[core], send_sem=ar_s.at[6], recv_sem=ar_r.at[6],
        device_id={"fine": place["partner"]}, device_id_type=MESH)
    pair_fin.start()
    ag1.wait(9)
    at_far = pl.multiple_of(y_far * 2 * cells, 2 * cells)

    @pl.loop(0, nodes // (2 * cells))
    def _(b):
        at = pl.ds(pl.multiple_of(b * 2 * cells, 2 * cells), 2 * cells)
        part = dot(unpool_mat[at, pl.ds(at_far, 2 * cells)], gp[pl.ds(at_far, 2 * cells), :])
        out_gf[at, :] = (go[at, :].astype(F32) + (acc[at, :] + part)).astype(BF16)

    pltpu.make_async_remote_copy(
        src_ref=w_ag, dst_ref=w_fin.at[1 - core], send_sem=ar_s.at[6], recv_sem=ar_r.at[6],
        device_id={"fine": place["partner"]}, device_id_type=MESH).wait_recv()
    out_w1[...] = w_fin[0, :, 0:feat].astype(F32) * edge_scale
    out_w2[...] = w_fin[1, 0:feat, 0:feat].astype(F32) * edge_scale
    out_w3[...] = w_fin[1, feat:2 * feat, 0:feat].astype(F32) * cell_scale
    for q in range(feat // L):
        out_b1[:, q * L:(q + 1) * L] = (
            w_fin[0, q * 16:q * 16 + 1, feat:].astype(F32) * edge_scale)

    for s in sc:
        s.drain()
    ag0.drain()
    ag1.drain()
    for q in range(2):
        halo_out(q).wait_send()
        halo_back(q).wait_send()
    pair_w.wait_send()
    many.wait_send()
    for t in (1, 2, 3):
        y_out(t).wait_send()
    many_back.wait_send()
    pair_fin.wait_send()


def local(
    node_feats, grad_out, cluster_ids, halo_lists, edge_sources,
    w_edge_in, b_edge_in, w_edge_out, w_unpool,
):
    nodes, feat = node_feats.shape
    group = edge_sources.shape[0] // K
    cells = group // 8
    edges = K * cells
    side = halo_lists.shape[0] // 2
    rows = group + 2 * side
    n_coarse = lax.axis_size("coarse")
    edge_scale = float(group * n_coarse * K) ** -0.5
    cell_scale = float(group * n_coarse) ** -0.5
    half = cells // 2
    piece = 2 * feat // n_coarse
    wide_feat = feat + L
    vmem = pltpu.VMEM
    dma = pltpu.SemaphoreType.DMA
    out = pl.pallas_call(
        functools.partial(kernel, n_coarse, edge_scale, cell_scale),
        out_shape=(
            jax.ShapeDtypeStruct((nodes, feat), BF16),
            jax.ShapeDtypeStruct((2 * feat, feat), F32),
            jax.ShapeDtypeStruct((1, feat), F32),
            jax.ShapeDtypeStruct((feat, feat), F32),
            jax.ShapeDtypeStruct((feat, feat), F32),
        ),
        in_specs=[pl.BlockSpec(memory_space=vmem)] * 9,
        out_specs=(pl.BlockSpec(memory_space=vmem),) * 5,
        scratch_shapes=[
            vmem((NY, 2 * cells, nodes), BF16),
            vmem((nodes, group), BF16),
            vmem((edges, rows), BF16),
            vmem((rows, edges), BF16),
            vmem((2 * side, group), BF16),
            vmem((group, 2 * side), BF16),
            vmem((edges, L), I32),
            vmem((edges // L, L), I32),
            vmem((NY, 2 * cells, feat), F32),
            vmem((NY, 2 * cells, feat), F32),
            vmem((NY, 2 * cells, feat), F32),
            vmem((3, NY, cells, feat), BF16),
            vmem((3, NY, cells, feat), BF16),
            vmem((3, 6, half, feat), BF16),
            vmem((3, 6, half, feat), BF16),
            vmem((rows, feat), BF16),
            vmem((group, feat), BF16),
            vmem((2, 2, side, feat), BF16),
            vmem((edges, feat), BF16),
            vmem((2 * side, feat), BF16),
            vmem((edges, feat), BF16),
            vmem((2 * cells, feat), F32),
            vmem((nodes, feat), F32),
            vmem((2, 2 * feat, wide_feat), F32),
            vmem((2 * feat, wide_feat), BF16),
            vmem((2 * feat, wide_feat), BF16),
            vmem((2 * feat, wide_feat), BF16),
            vmem(((n_coarse - 1) * piece, wide_feat), BF16),
            vmem((NY, piece, wide_feat), BF16),
            vmem((2 * feat, wide_feat), BF16),
            vmem((2, 2 * feat, wide_feat), BF16),
            dma((3, NY)), dma((3, NY)), dma((3, 6)), dma((3, 6)),
            dma((2, 10)), dma((2, 10)),
            dma((4,)), dma((4,)),
            dma((7,)), dma((7,)),
        ],
        compiler_params=pltpu.CompilerParams(
            collective_id=0, has_side_effects=True, vmem_limit_bytes=60 * 2**20),
    )(
        node_feats, grad_out,
        cluster_ids.reshape(nodes // L, L),
        halo_lists.reshape(2, side),
        edge_sources.reshape(group * K // L, L),
        w_edge_in, b_edge_in.reshape(1, feat), w_edge_out, w_unpool,
    )
    return out[0], out[1], out[2].reshape(feat), out[3], out[4]


def solution(mesh):
    return jax.shard_map(
        local,
        mesh=mesh,
        in_specs=(
            P(("coarse", "fine"), None), P(("coarse", "fine"), None), P(("coarse", "fine")),
            P("coarse"), P("coarse"), P(), P(), P(), P(),
        ),
        out_specs=(P(("coarse", "fine"), None), P(), P(), P(), P()),
        check_vma=False,
    )
```

```python
import functools

import jax
import jax.numpy as jnp
from jax import lax
from jax.experimental import pallas as pl
from jax.experimental.pallas import tpu as pltpu
from jax.sharding import PartitionSpec as P

MESH = pl.DeviceIdType.MESH
F32 = jnp.float32
BF16 = jnp.bfloat16
I32 = jnp.int32
K = 4
NY = 4
L = 128


def dot(a, b, dims=((1,), (0,))):
    return lax.dot_general(a, b, (dims, ((), ())), preferred_element_type=F32)


def onehot(mask):
    return jnp.where(mask, 1.0, 0.0).astype(BF16)


def columns(row):
    return jnp.transpose(jnp.broadcast_to(row, (L, L)))


class Scatter:
    def __init__(self, place, stage, psend, prcv, ysend, yrcv, sems):
        self.p = place
        self.stage, self.psend, self.prcv = stage, psend, prcv
        self.ysend, self.yrcv = ysend, yrcv
        self.ps, self.pr, self.ys, self.yr = sems
        self.cells = psend.shape[1]

    def pair(self, r):
        return pltpu.make_async_remote_copy(
            src_ref=self.psend.at[r], dst_ref=self.prcv.at[r],
            send_sem=self.ps.at[r], recv_sem=self.pr.at[r],
            device_id={"fine": self.p["partner"]}, device_id_type=MESH)

    def ring(self, r):
        return pltpu.make_async_remote_copy(
            src_ref=self.ysend.at[r - 1], dst_ref=self.yrcv.at[r - 1],
            send_sem=self.ys.at[r - 1], recv_sem=self.yr.at[r - 1],
            device_id={"fine": self.p["step"][r]}, device_id_type=MESH)

    def emit_pair(self, r):
        at = pl.multiple_of((1 - self.p["core"]) * self.cells, self.cells)
        self.psend[r] = self.stage[r, pl.ds(at, self.cells), :].astype(BF16)
        self.pair(r).start()

    def chip_sum(self, r):
        self.pair(r).wait_recv()
        at = pl.multiple_of(self.p["core"] * self.cells, self.cells)
        return self.stage[r, pl.ds(at, self.cells), :] + self.prcv[r].astype(F32)

    def send(self, r):
        self.ysend[r - 1] = self.chip_sum(r).astype(BF16)
        self.ring(r).start()

    def finish(self):
        total = self.chip_sum(0)
        for r in (1, 3, 2):
            self.ring(r).wait_recv()
            total = total + self.yrcv[r - 1].astype(F32)
        return total

    def drain(self):
        for r in range(NY):
            self.pair(r).wait_send()
        for r in (1, 2, 3):
            self.ring(r).wait_send()


class Gather:
    def __init__(self, place, table, cells, sems):
        self.p, self.table, self.cells = place, table, cells
        self.ss, self.rs = sems

    def copy(self, i, to, y, core):
        at = pl.multiple_of((y * 2 + core) * self.cells, self.cells)
        ref = self.table.at[pl.ds(at, self.cells), :]
        return pltpu.make_async_remote_copy(
            src_ref=ref, dst_ref=ref, send_sem=self.ss.at[i], recv_sem=self.rs.at[i],
            device_id={"fine": to}, device_id_type=MESH)

    def out(self, i):
        p, c = self.p, self.p["core"]
        if i < NY:
            return self.copy(i, p["step"][i] if i else p["partner"], p["ys"][0], c)
        return self.copy(i, p["partner"], p["ys"][(NY - (i - 3)) % NY], c)

    def arrival(self, i):
        p, c = self.p, self.p["core"]
        if i == 0:
            return self.copy(i, p["partner"], p["ys"][0], 1 - c)
        if i < NY:
            return self.copy(i, p["partner"], p["ys"][NY - i], c)
        return self.copy(i, p["partner"], p["ys"][(NY - (i - 3)) % NY], 1 - c)

    def start(self):
        for i in (2, 1, 3, 0):
            self.out(i).start()

    def share(self, i):
        self.arrival(i).wait_recv()
        self.out(i + 3).start()

    def wait(self, *which):
        for i in which:
            self.arrival(i).wait_recv()

    def drain(self):
        for i in range(7):
            self.out(i).wait_send()


def kernel(
    n_coarse, edge_scale, cell_scale,
    cid, halo, es, b1, nf_hbm, go_hbm, w1_hbm, w2_hbm, w3_hbm,
    out_gf, out_w1, out_b1, out_w2, out_w3,
    nf, go, w1, w2, w3,
    pool_mat, unpool_mat, src_mat, src_mat_t, halo_mat, halo_mat_t,
    es_col, es_row,
    st0, st1, st2, psend, prcv, ysend, yrcv,
    ext, gp, hsend, gret, back, turned, hid, slope, wide, acc,
    w_part, w_pair_s, w_pair_r, w_rs_s, w_rs_r, w_y, w_ag, w_fin, tally,
    ins, ps, pr, ys, yr, ags, agr, hs_s, hs_r, ar_s, ar_r,
):
    cells = gp.shape[0] // 8
    group = 8 * cells
    nodes, feat = nf.shape
    edges = K * cells
    side = halo.shape[1]
    rows = group + 2 * side
    n_bias = feat // L
    g = lax.axis_index("coarse")
    f = lax.axis_index("fine")
    core = lax.rem(f, 2)
    y = lax.div(f, 2)
    y_of = tuple(lax.rem(y + r, NY) for r in range(NY))
    place = {
        "core": core, "ys": y_of, "partner": f + 1 - 2 * core,
        "step": tuple(y_r * 2 + core for y_r in y_of),
    }
    right, left = lax.rem(g + 1, n_coarse), lax.rem(g + n_coarse - 1, n_coarse)

    loads = [
        pltpu.make_async_copy(a, b, ins.at[i])
        for i, (a, b) in enumerate(
            ((nf_hbm, nf), (go_hbm, go), (w1_hbm, w1), (w2_hbm, w2), (w3_hbm, w3)))
    ]
    for load in loads:
        load.start()
    w_ag[:, feat:] = jnp.zeros((2 * feat, L), BF16)

    barrier = pltpu.get_barrier_semaphore()
    for to in (place["partner"],) + place["step"][1:]:
        pl.semaphore_signal(barrier, inc=1, device_id={"fine": to}, device_id_type=MESH)

    @pl.loop(1, n_coarse)
    def _(t):
        pl.semaphore_signal(
            barrier, inc=1, device_id={"coarse": lax.rem(g + t, n_coarse)}, device_id_type=MESH)

    own = pl.multiple_of(f * cells, cells)

    def pair_rows(r):
        return pl.multiple_of(y_of[r] * 2 * cells, 2 * cells)

    def build_pool(r):
        ids = lax.broadcasted_iota(I32, (2 * cells, L), 0) + (g * group + y_of[r] * 2 * cells)

        for b in range(nodes // L):
            pool_mat[r, :, b * L:(b + 1) * L] = onehot(ids == cid[b:b + 1, :])

    sc = [
        Scatter(place, st, psend.at[i], prcv.at[i], ysend.at[i], yrcv.at[i],
                (ps.at[i], pr.at[i], ys.at[i], yr.at[i]))
        for i, st in enumerate((st0, st1, st2))
    ]
    ag0 = Gather(place, ext, cells, (ags.at[0], agr.at[0]))
    ag1 = Gather(place, gp, cells, (ags.at[1], agr.at[1]))

    def pool(r, x, stage):
        stage[r] = dot(pool_mat[r], x[...])

    build_pool(2)
    loads[0].wait()
    pool(2, nf, st0)
    build_pool(1)
    pl.semaphore_wait(barrier, 4 + n_coarse - 1)
    sc[0].emit_pair(2)
    pool(1, nf, st0)
    build_pool(3)
    sc[0].emit_pair(1)
    sc[0].send(2)
    pool(3, nf, st0)
    build_pool(0)
    sc[0].emit_pair(3)
    sc[0].send(1)
    pool(0, nf, st0)
    sc[0].emit_pair(0)
    sc[0].send(3)
    loads[1].wait()
    for r in (2, 1, 3, 0):
        pool(r, go, st1)
        sc[1].emit_pair(r)

    total = sc[0].finish()
    wide[0:cells] = total
    ext[pl.ds(own, cells), :] = total.astype(BF16)
    ag0.start()
    turned[0:feat, :] = jnp.concatenate([jnp.transpose(total.astype(BF16))] * K, axis=1)

    at_es = pl.multiple_of(f * (edges // L), edges // L)

    @pl.loop(0, edges // L)
    def _(b):
        es_col[pl.ds(pl.multiple_of(b * L, L), L), :] = columns(es[pl.ds(at_es + b, 1), :])

    lane = lax.broadcasted_iota(I32, (L, L), 1)
    sub = lax.broadcasted_iota(I32, (L, L), 0)
    for q in range(2):
        col = columns(halo[q:q + 1, :])

        @pl.loop(0, group // L)
        def _(j, col=col, q=q):
            halo_mat[q * L:(q + 1) * L, pl.ds(pl.multiple_of(j * L, L), L)] = onehot(
                col == lane + j * L)

    for k in range(K):
        for q in range(cells // L):
            at = k * cells + q * L
            col = es_col[pl.ds(k + q * L * K, L, stride=K), :]
            es_row[at // L:at // L + 1, :] = jnp.transpose(col)[0:1, :]

            @pl.loop(0, rows // L)
            def _(j, col=col, at=at):
                src_mat[at:at + L, pl.ds(pl.multiple_of(j * L, L), L)] = onehot(col == lane + j * L)

    ag0.share(1)
    ag0.share(3)
    ag0.share(2)
    for r in (2, 1, 3):
        sc[1].send(r)

    @pl.loop(0, group // L)
    def _(j):
        at = pl.multiple_of(j * L, L)
        for q in range(2):
            halo_mat_t[pl.ds(at, L), q * L:(q + 1) * L] = onehot(halo[q:q + 1, :] == sub + j * L)

    ag0.wait(0, 4, 6, 5)

    def halo_out(q):
        to, row = (right, 0) if q == 0 else (left, side)
        at = group + row
        return pltpu.make_async_remote_copy(
            src_ref=hsend.at[0, q], dst_ref=ext.at[at:at + side, :],
            send_sem=hs_s.at[q], recv_sem=hs_r.at[q],
            device_id={"coarse": to}, device_id_type=MESH)

    picked = dot(halo_mat[...], ext[0:group, :])
    hsend[0, 0] = picked[0:side].astype(BF16)
    hsend[0, 1] = picked[side:2 * side].astype(BF16)
    halo_out(0).start()
    halo_out(1).start()

    acc[0:edges, :] = dot(src_mat[:, 0:group], ext[0:group, :])

    @pl.loop(0, rows // L)
    def _(j):
        at = pl.multiple_of(j * L, L)
        for b in range(edges // L):
            src_mat_t[pl.ds(at, L), b * L:(b + 1) * L] = onehot(es_row[b:b + 1, :] == sub + j * L)

    for load in loads[2:]:
        load.wait()
    pooled_bf = wide[0:cells].astype(BF16)
    bias_row = jnp.concatenate([b1[q:q + 1, :].astype(F32) for q in range(n_bias)], axis=1)
    pre_dst = dot(pooled_bf, w1[0:feat, :]) + bias_row
    halo_out(0).wait_recv()
    halo_out(1).wait_recv()
    src_feats = (
        acc[0:edges, :] + dot(src_mat[:, group:rows], ext[group:rows, :])
    ).astype(BF16)
    acc[0:edges, :] = dot(src_feats, w1[feat:2 * feat, :])
    turned[feat:, :] = jnp.transpose(src_feats)

    spans = [slice(k * cells, (k + 1) * cells) for k in range(K)]
    new_coarse = wide[0:cells]
    for span in spans:
        pre = pre_dst + acc[span, :]
        sig = 1.0 / (1.0 + jnp.exp(-pre))
        hidden = (pre * sig).astype(BF16)
        hid[span, :] = hidden
        slope[span, :] = sig * (1.0 + pre * (1.0 - sig))
        new_coarse = new_coarse + dot(hidden, w2[...])
    new_coarse = new_coarse.astype(BF16)

    last = ((1,), (1,))
    gsum = sc[1].finish().astype(BF16)
    gnew = dot(gsum, w3[...], last).astype(BF16)
    ghid = dot(gnew, w2[...], last)
    act_sum = jnp.zeros((cells, feat), F32)
    for span in spans:
        act = (ghid * slope[span, :]).astype(BF16)
        gret[span, :] = act
        act_sum = act_sum + act.astype(F32)

    def halo_back(q):
        to = left if q == 0 else right
        return pltpu.make_async_remote_copy(
            src_ref=hsend.at[1, q], dst_ref=back.at[pl.ds(q * side, side), :],
            send_sem=hs_s.at[2 + q], recv_sem=hs_r.at[2 + q],
            device_id={"coarse": to}, device_id_type=MESH)

    outer = dot(src_mat_t[group:rows, :], gret[...])
    hsend[1, 0] = outer[0:side].astype(BF16)
    hsend[1, 1] = outer[side:2 * side].astype(BF16)
    halo_back(0).start()
    halo_back(1).start()

    w_part[0, :, 0:feat] = dot(turned[...], gret[...])
    gnew_t = jnp.concatenate([jnp.transpose(gnew)] * K, axis=1)
    w_part[1, 0:feat, 0:feat] = jnp.transpose(dot(gnew_t, hid[...]))
    w_part[1, feat:2 * feat, 0:feat] = dot(new_coarse, gsum, ((0,), (0,)))
    w_part[:, :, feat:] = jnp.zeros((2, 2 * feat, L), F32)
    piece = w_rs_s.shape[0] // n_coarse
    bias = jnp.sum(act_sum, axis=0, keepdims=True)
    for q in range(n_bias):
        w_part[0, q * piece:q * piece + 1, feat:] = bias[:, q * L:(q + 1) * L]

    pair_w = pltpu.make_async_remote_copy(
        src_ref=w_pair_s, dst_ref=w_pair_r, send_sem=ar_s.at[0], recv_sem=ar_r.at[0],
        device_id={"fine": place["partner"]}, device_id_type=MESH)
    w_pair_s[...] = w_part[1 - core].astype(BF16)
    pair_w.start()

    def spread(r):
        st2[r] = dot(src_mat_t[pl.ds(pair_rows(r), 2 * cells), :], gret[...])

    spread(2)
    spread(1)
    pair_w.wait_recv()
    w_rs_s[...] = (w_part[core] + w_pair_r[...].astype(F32)).astype(BF16)

    def far_first(i):
        return n_coarse // 2 + (i + 1) // 2 * (1 - 2 * (i % 2))

    def piece_out(t, width):
        j = lax.rem(g + t, n_coarse)
        return pltpu.make_async_remote_copy(
            src_ref=w_rs_s.at[pl.ds(pl.multiple_of(j * piece, piece), piece), 0:width],
            dst_ref=w_rs_r.at[
                pl.ds(pl.multiple_of((n_coarse - 1 - t) * piece, piece), piece), 0:width],
            send_sem=ar_s.at[1], recv_sem=ar_r.at[1],
            device_id={"coarse": j}, device_id_type=MESH)

    @pl.loop(0, n_coarse - 1)
    def _(i):
        t = far_first(i)
        wide_piece = lax.rem(g + t, n_coarse) < n_bias

        @pl.when(wide_piece)
        def _():
            piece_out(t, feat + L).start()

        @pl.when(jnp.logical_not(wide_piece))
        def _():
            piece_out(t, feat).start()

    spread(3)
    spread(0)
    halo_back(0).wait_recv()
    halo_back(1).wait_recv()

    def add_back(r):
        st2[r] = st2[r] + dot(halo_mat_t[pl.ds(pair_rows(r), 2 * cells), :], back[...])
        sc[2].emit_pair(r)

    add_back(2)
    add_back(1)
    sc[2].send(2)
    add_back(3)
    sc[2].send(1)
    add_back(0)
    sc[2].send(3)

    @pl.loop(0, nodes // L)
    def _(b):
        col = columns(cid[pl.ds(b, 1), :])
        at = pl.multiple_of(b * L, L)
        for j in range(group // L):
            unpool_mat[pl.ds(at, L), j * L:(j + 1) * L] = onehot(
                col == lane + (g * group + j * L))

    carries = g < n_bias
    plain = jnp.logical_not(carries)
    n_tiles = 2 * (n_coarse - 1) + n_bias

    def several(width, at):
        ref = w_rs_r.at[:, 0:width]
        return pltpu.make_async_remote_copy(
            src_ref=ref, dst_ref=ref, send_sem=ar_s.at[at], recv_sem=ar_r.at[at],
            device_id={"coarse": right}, device_id_type=MESH)

    def mixed(tiles, at):
        ref = tally.at[0:tiles * piece, :]
        return pltpu.make_async_remote_copy(
            src_ref=ref, dst_ref=ref, send_sem=ar_s.at[at], recv_sem=ar_r.at[at],
            device_id={"coarse": right}, device_id_type=MESH)

    my_piece = pl.multiple_of(g * piece, piece)

    def piece_sum(span):
        total = w_rs_s[pl.ds(my_piece, piece), span].astype(F32)
        for t in range(n_coarse - 1):
            total = total + w_rs_r[t * piece:(t + 1) * piece, span].astype(F32)
        return total

    @pl.when(carries)
    def _():
        several(feat + L, 1).wait_recv()
        w_y[y, :, feat:] = piece_sum(slice(feat, feat + L))

    @pl.when(plain)
    def _():
        several(feat, 1).wait_recv()
        w_y[y, :, feat:] = jnp.zeros((piece, L), F32)

    w_y[y, :, 0:feat] = piece_sum(slice(0, feat))

    def y_copy(t, at):
        return pltpu.make_async_remote_copy(
            src_ref=w_y.at[at], dst_ref=w_y.at[at], send_sem=ar_s.at[1 + t],
            recv_sem=ar_r.at[1 + t], device_id={"fine": place["step"][t]}, device_id_type=MESH)

    for t in (2, 1, 3):
        y_copy(t, y).start()

    gpool = gnew.astype(F32)
    for k in range(K):
        gpool = gpool + dot(gret[k * cells:(k + 1) * cells, :], w1[0:feat, :], last)
    src_grad = sc[2].finish().astype(BF16)
    gpool = gpool + dot(src_grad, w1[feat:, :], last)
    gp[pl.ds(own, cells), :] = gpool.astype(BF16)
    ag1.start()

    def take(y_at, first_pass):
        at = pl.multiple_of(y_at * 2 * cells, 2 * cells)
        part = dot(unpool_mat[:, pl.ds(at, 2 * cells)], gp[pl.ds(at, 2 * cells), :])
        if first_pass:
            acc[...] = part
        else:
            acc[...] += part

    ag1.wait(0)
    take(y, True)

    for t in (1, 2, 3):
        y_copy(t, y_of[NY - t]).wait_recv()
    summed = w_y[0]
    for t in range(1, NY):
        summed = summed + w_y[t]
    w_ag[pl.ds(my_piece, piece), :] = summed.astype(BF16)

    def piece_back(t, width):
        ref = w_ag.at[pl.ds(my_piece, piece), 0:width]
        return pltpu.make_async_remote_copy(
            src_ref=ref, dst_ref=ref, send_sem=ar_s.at[5], recv_sem=ar_r.at[5],
            device_id={"coarse": lax.rem(g + t, n_coarse)}, device_id_type=MESH)

    @pl.when(carries)
    def _():
        @pl.loop(0, n_coarse - 1)
        def _(i):
            piece_back(far_first(i), feat + L).start()

    @pl.when(plain)
    def _():
        @pl.loop(0, n_coarse - 1)
        def _(i):
            piece_back(far_first(i), feat).start()

    ag1.share(1)
    ag1.share(3)
    ag1.share(2)
    ag1.wait(4)
    take(y_of[3], False)
    ag1.wait(6)
    take(y_of[1], False)
    ag1.wait(5)
    at_far = pair_rows(2)

    @pl.loop(0, nodes // (2 * cells))
    def _(b):
        at = pl.ds(pl.multiple_of(b * 2 * cells, 2 * cells), 2 * cells)
        part = dot(unpool_mat[at, pl.ds(at_far, 2 * cells)], gp[pl.ds(at_far, 2 * cells), :])
        out_gf[at, :] = (go[at, :].astype(F32) + (acc[at, :] + part)).astype(BF16)

    @pl.when(carries)
    def _():
        mixed(n_tiles - 1, 5).wait_recv()

    @pl.when(plain)
    def _():
        mixed(n_tiles, 5).wait_recv()

    w_fin[core] = w_ag[...]
    pair_fin = pltpu.make_async_remote_copy(
        src_ref=w_ag, dst_ref=w_fin.at[core], send_sem=ar_s.at[6], recv_sem=ar_r.at[6],
        device_id={"fine": place["partner"]}, device_id_type=MESH)
    pair_fin.start()

    for s in sc:
        s.drain()
    ag0.drain()
    ag1.drain()
    for q in range(2):
        halo_out(q).wait_send()
        halo_back(q).wait_send()
    pair_w.wait_send()

    @pl.when(carries)
    def _():
        mixed(n_tiles - 1, 1).wait_send()
        several(feat + L, 5).wait_send()

    @pl.when(plain)
    def _():
        mixed(n_tiles, 1).wait_send()
        several(feat, 5).wait_send()

    for t in (1, 2, 3):
        y_copy(t, y).wait_send()
    pair_fin.wait_send()
    pltpu.make_async_remote_copy(
        src_ref=w_ag, dst_ref=w_fin.at[1 - core], send_sem=ar_s.at[6], recv_sem=ar_r.at[6],
        device_id={"fine": place["partner"]}, device_id_type=MESH).wait_recv()
    out_w1[...] = w_fin[0, :, 0:feat].astype(F32) * edge_scale
    out_w2[...] = w_fin[1, 0:feat, 0:feat].astype(F32) * edge_scale
    out_w3[...] = w_fin[1, feat:2 * feat, 0:feat].astype(F32) * cell_scale
    for q in range(n_bias):
        out_b1[:, q * L:(q + 1) * L] = (
            w_fin[0, q * piece:q * piece + 1, feat:].astype(F32) * edge_scale)


def store(*refs):
    count = (len(refs) - 1) // 2
    copies = [
        pltpu.make_async_copy(refs[i], refs[count + i], refs[-1].at[i]) for i in range(count)
    ]
    for copy in copies:
        copy.start()
    for copy in copies:
        copy.wait()


def local(
    node_feats, grad_out, cluster_ids, halo_lists, edge_sources,
    w_edge_in, b_edge_in, w_edge_out, w_unpool,
):
    nodes, feat = node_feats.shape
    group = edge_sources.shape[0] // K
    cells = group // 8
    edges = K * cells
    side = halo_lists.shape[0] // 2
    rows = group + 2 * side
    n_coarse = lax.axis_size("coarse")
    edge_scale = float(group * n_coarse * K) ** -0.5
    cell_scale = float(group * n_coarse) ** -0.5
    piece = 2 * feat // n_coarse
    n_tiles = 2 * (n_coarse - 1) + feat // L
    wide_feat = feat + L
    vmem = pltpu.VMEM
    dma = pltpu.SemaphoreType.DMA
    results = (
        ((nodes, feat), BF16), ((2 * feat, feat), F32), ((1, feat), F32),
        ((feat, feat), F32), ((feat, feat), F32),
    )
    in_vmem = pl.BlockSpec(memory_space=vmem)
    anywhere = pl.BlockSpec(memory_space=pl.ANY)
    parts = pl.pallas_call(
        functools.partial(kernel, n_coarse, edge_scale, cell_scale),
        out_shape=tuple(pltpu.VMEM(shape, kind) for shape, kind in results),
        in_specs=[in_vmem] * 4 + [anywhere] * 5,
        out_specs=(in_vmem,) * 5,
        scratch_shapes=[
            vmem((nodes, feat), BF16),
            vmem((nodes, feat), BF16),
            vmem((2 * feat, feat), BF16),
            vmem((feat, feat), BF16),
            vmem((feat, feat), BF16),
            vmem((NY, 2 * cells, nodes), BF16),
            vmem((nodes, group), BF16),
            vmem((edges, rows), BF16),
            vmem((rows, edges), BF16),
            vmem((2 * side, group), BF16),
            vmem((group, 2 * side), BF16),
            vmem((edges, L), I32),
            vmem((edges // L, L), I32),
            vmem((NY, 2 * cells, feat), F32),
            vmem((NY, 2 * cells, feat), F32),
            vmem((NY, 2 * cells, feat), F32),
            vmem((3, NY, cells, feat), BF16),
            vmem((3, NY, cells, feat), BF16),
            vmem((3, 3, cells, feat), BF16),
            vmem((3, 3, cells, feat), BF16),
            vmem((rows, feat), BF16),
            vmem((group, feat), BF16),
            vmem((2, 2, side, feat), BF16),
            vmem((edges, feat), BF16),
            vmem((2 * side, feat), BF16),
            vmem((2 * feat, edges), BF16),
            vmem((edges, feat), BF16),
            vmem((edges, feat), F32),
            vmem((2 * cells, feat), F32),
            vmem((nodes, feat), F32),
            vmem((2, 2 * feat, wide_feat), F32),
            vmem((2 * feat, wide_feat), BF16),
            vmem((2 * feat, wide_feat), BF16),
            vmem((2 * feat, wide_feat), BF16),
            vmem(((n_coarse - 1) * piece, wide_feat), BF16),
            vmem((NY, piece, wide_feat), F32),
            vmem((2 * feat, wide_feat), BF16),
            vmem((2, 2 * feat, wide_feat), BF16),
            vmem((n_tiles * piece, L), BF16),
            dma((5,)),
            dma((3, NY)), dma((3, NY)), dma((3, 3)), dma((3, 3)),
            dma((2, 7)), dma((2, 7)),
            dma((4,)), dma((4,)),
            dma((7,)), dma((7,)),
        ],
        compiler_params=pltpu.CompilerParams(
            collective_id=0, has_side_effects=True, vmem_limit_bytes=58 * 2**20),
    )(
        cluster_ids.reshape(nodes // L, L),
        halo_lists.reshape(2, side),
        edge_sources.reshape(group * K // L, L),
        b_edge_in.reshape(feat // L, L),
        node_feats, grad_out, w_edge_in, w_edge_out, w_unpool,
    )
    out = pl.pallas_call(
        store,
        out_shape=tuple(jax.ShapeDtypeStruct(shape, kind) for shape, kind in results),
        in_specs=[anywhere] * 5,
        out_specs=(anywhere,) * 5,
        scratch_shapes=[dma((5,))],
        compiler_params=pltpu.CompilerParams(vmem_limit_bytes=2**20),
    )(*[pltpu.with_memory_space_constraint(part, pltpu.VMEM) for part in parts])
    return out[0], out[1], out[2].reshape(feat), out[3], out[4]


def solution(mesh):
    return jax.shard_map(
        local,
        mesh=mesh,
        in_specs=(
            P(("coarse", "fine"), None), P(("coarse", "fine"), None), P(("coarse", "fine")),
            P("coarse"), P("coarse"), P(), P(), P(), P(),
        ),
        out_specs=(P(("coarse", "fine"), None), P(), P(), P(), P()),
        check_vma=False,
    )
```

```python
import functools

import jax
import jax.numpy as jnp
from jax import lax
from jax.experimental import pallas as pl
from jax.experimental.pallas import tpu as pltpu
from jax.sharding import PartitionSpec as P

MESH = pl.DeviceIdType.MESH
F32 = jnp.float32
BF16 = jnp.bfloat16
I32 = jnp.int32
K = 4
NY = 4
L = 128


def dot(a, b, dims=((1,), (0,))):
    return lax.dot_general(a, b, (dims, ((), ())), preferred_element_type=F32)


def onehot(mask):
    return jnp.where(mask, 1.0, 0.0).astype(BF16)


def onehot16(mask):
    return jnp.where(mask, jnp.ones((), BF16), jnp.zeros((), BF16))


def columns(row):
    return jnp.transpose(jnp.broadcast_to(row, (L, L)))


class Scatter:
    def __init__(self, place, stage, psend, prcv, ysend, yrcv, sems, lots=1):
        self.p = place
        self.stage, self.psend, self.prcv = stage, psend, prcv
        self.ysend, self.yrcv = ysend, yrcv
        self.ps, self.pr, self.ys, self.yr = sems
        self.cells = psend.shape[1]
        self.lots, self.rows = lots, psend.shape[1] // lots

    def part(self, q):
        return pl.ds(q * self.rows, self.rows)

    def pair(self, r, q):
        return pltpu.make_async_remote_copy(
            src_ref=self.psend.at[r, self.part(q)], dst_ref=self.prcv.at[r, self.part(q)],
            send_sem=self.ps.at[r, q], recv_sem=self.pr.at[r, q],
            device_id={"fine": self.p["partner"]}, device_id_type=MESH)

    def ring(self, r, q):
        return pltpu.make_async_remote_copy(
            src_ref=self.ysend.at[r - 1, self.part(q)], dst_ref=self.yrcv.at[r - 1, self.part(q)],
            send_sem=self.ys.at[r - 1, q], recv_sem=self.yr.at[r - 1, q],
            device_id={"fine": self.p["step"][r]}, device_id_type=MESH)

    def emit_pair(self, r):
        at = pl.multiple_of((1 - self.p["core"]) * self.cells, self.cells)
        self.psend[r] = self.stage[r, pl.ds(at, self.cells), :].astype(BF16)
        for q in range(self.lots):
            self.pair(r, q).start()

    def chip_sum(self, r, q):
        self.pair(r, q).wait_recv()
        at = pl.multiple_of(self.p["core"] * self.cells + q * self.rows, self.rows)
        return self.stage[r, pl.ds(at, self.rows), :] + self.prcv[r, self.part(q)].astype(F32)

    def send(self, r, q=0):
        self.ysend[r - 1, self.part(q)] = self.chip_sum(r, q).astype(BF16)
        self.ring(r, q).start()

    def finish(self, q=0):
        total = self.chip_sum(0, q)
        for r in (1, 3, 2):
            self.ring(r, q).wait_recv()
            total = total + self.yrcv[r - 1, self.part(q)].astype(F32)
        return total

    def drain(self):
        for q in range(self.lots):
            for r in range(NY):
                self.pair(r, q).wait_send()
            for r in (1, 2, 3):
                self.ring(r, q).wait_send()


class Gather:
    def __init__(self, place, table, cells, sems, lots=1):
        self.p, self.table, self.cells = place, table, cells
        self.lots, self.rows = lots, cells // lots
        self.ss, self.rs = sems

    def copy(self, i, q, to, y, core):
        at = pl.multiple_of((y * 2 + core) * self.cells + q * self.rows, self.rows)
        ref = self.table.at[pl.ds(at, self.rows), :]
        return pltpu.make_async_remote_copy(
            src_ref=ref, dst_ref=ref, send_sem=self.ss.at[i, q], recv_sem=self.rs.at[i, q],
            device_id={"fine": to}, device_id_type=MESH)

    def out(self, i, q):
        p, c = self.p, self.p["core"]
        if i < NY:
            return self.copy(i, q, p["step"][i] if i else p["partner"], p["ys"][0], c)
        return self.copy(i, q, p["partner"], p["ys"][(NY - (i - 3)) % NY], c)

    def arrival(self, i, q):
        p, c = self.p, self.p["core"]
        if i == 0:
            return self.copy(i, q, p["partner"], p["ys"][0], 1 - c)
        if i < NY:
            return self.copy(i, q, p["partner"], p["ys"][NY - i], c)
        return self.copy(i, q, p["partner"], p["ys"][(NY - (i - 3)) % NY], 1 - c)

    def start(self, q=0):
        for i in (2, 1, 3, 0):
            self.out(i, q).start()

    def share(self, i, q=0):
        self.arrival(i, q).wait_recv()
        self.out(i + 3, q).start()

    def wait(self, *which):
        for q in range(self.lots):
            for i in which:
                self.arrival(i, q).wait_recv()

    def drain(self):
        for q in range(self.lots):
            for i in range(7):
                self.out(i, q).wait_send()


def kernel(
    n_coarse, nx, edge_scale, cell_scale,
    cid_hbm, halo_hbm, es_hbm, b1_hbm, nf_hbm, go_hbm, w1_hbm, w2_hbm, w3_hbm,
    out_gf, out_w1, out_b1, out_w2, out_w3,
    cid, halo, es, b1, nf, go, w1, w2, w3,
    pool_mat, unpool_mat, src_mat, src_mat_t, halo_mat, list_mat,
    es_col, es_row,
    st0, st1, st2, psend, prcv, ysend, yrcv,
    st3, psend3, prcv3, ysend3, yrcv3, hb,
    ext, gp, hsend, gret, back, turned, hid, slope, wide, acc,
    w_part, w_pair_s, w_pair_r, w_rs, w_x, w_own, w_z_s, w_z_r, w_y, w_ag, w_fin,
    b_pair_s, b_pair_r, b_x, b_z, b_y,
    ins, ps, pr, ys, yr, ags, agr, hs_s, hs_r, ar_s, ar_r, br_s, br_r,
):
    cells = gp.shape[0] // 8
    group = 8 * cells
    nodes, feat = nf.shape
    edges = K * cells
    side = halo.shape[1]
    rows = group + 2 * side
    n_bias = feat // L
    g = lax.axis_index("coarse")
    f = lax.axis_index("fine")
    core = lax.rem(f, 2)
    y = lax.div(f, 2)
    y_of = tuple(lax.rem(y + r, NY) for r in range(NY))
    place = {
        "core": core, "ys": y_of, "partner": f + 1 - 2 * core,
        "step": tuple(y_r * 2 + core for y_r in y_of),
    }
    right, left = lax.rem(g + 1, n_coarse), lax.rem(g + n_coarse - 1, n_coarse)

    nz = n_coarse // nx
    z, x = lax.div(g, nx), lax.rem(g, nx)
    x_peer = [z * nx + lax.rem(x + d, nx) for d in range(nx)]
    z_peer = [lax.rem(z + d, nz) * nx + x for d in range(nz)]

    quarter = nodes // 4
    first_loads = [pltpu.make_async_copy(cid_hbm, cid, ins.at[4])] + [
        pltpu.make_async_copy(
            nf_hbm.at[pl.ds(i * quarter, quarter), :], nf.at[pl.ds(i * quarter, quarter), :],
            ins.at[5 + i])
        for i in range(4)
    ]
    for load in first_loads:
        load.start()
    barrier = pltpu.get_barrier_semaphore()
    fine_peers = (place["partner"],) + place["step"][1:]
    coarse_peers = [right, left] + x_peer[1:] + z_peer[1:]
    for to in fine_peers:
        pl.semaphore_signal(barrier, inc=1, device_id={"fine": to}, device_id_type=MESH)
    for to in coarse_peers:
        pl.semaphore_signal(barrier, inc=1, device_id={"coarse": to}, device_id_type=MESH)
    loads = [
        pltpu.make_async_copy(a, b, ins.at[i])
        for i, (a, b) in enumerate(
            ((go_hbm, go), (w1_hbm, w1), (w2_hbm, w2), (w3_hbm, w3)))
    ] + [
        pltpu.make_async_copy(a, b, ins.at[9 + i])
        for i, (a, b) in enumerate(((halo_hbm, halo), (es_hbm, es), (b1_hbm, b1)))
    ]
    for load in loads:
        load.start()

    own = pl.multiple_of(f * cells, cells)

    def pair_rows(r):
        return pl.multiple_of(y_of[r] * 2 * cells, 2 * cells)

    cell_ids = lax.broadcasted_iota(I32, (2 * cells, L), 0).astype(jnp.int16)

    def build_pool(r):
        base = g * group + y_of[r] * 2 * cells
        for b in range(nodes // L):
            row = jnp.broadcast_to(cid[b:b + 1, :] - base, (16, L)).astype(jnp.int16)
            pool_mat[r, :, b * L:(b + 1) * L] = onehot16(
                cell_ids == jnp.concatenate([row] * (2 * cells // 16), axis=0))

    sc = [
        Scatter(place, st, psend.at[i], prcv.at[i], ysend.at[i], yrcv.at[i],
                (ps.at[i], pr.at[i], ys.at[i], yr.at[i]), 1 if i == 1 else 2)
        for i, st in enumerate((st0, st1, st2))
    ]
    sc.append(Scatter(place, st3, psend3, prcv3, ysend3, yrcv3,
                      (ps.at[3], pr.at[3], ys.at[3], yr.at[3])))
    ag0 = Gather(place, ext, cells, (ags.at[0], agr.at[0]), 2)
    ag1 = Gather(place, gp, cells, (ags.at[1], agr.at[1]), 2)
    share = hb.shape[0] // 8
    ag2 = Gather(place, hb, share, (ags.at[2], agr.at[2]))

    def pool(r, x, stage):
        stage[r] = dot(pool_mat[r], x[...])

    first_loads[0].wait()
    build_pool(2)
    for load in first_loads[1:]:
        load.wait()
    pool(2, nf, st0)
    pl.semaphore_wait(barrier, len(fine_peers) + len(coarse_peers))
    sc[0].emit_pair(2)
    build_pool(1)
    pool(1, nf, st0)
    sc[0].emit_pair(1)
    sc[0].send(2, 0)
    build_pool(3)
    pool(3, nf, st0)
    sc[0].emit_pair(3)
    sc[0].send(1, 0)
    build_pool(0)
    pool(0, nf, st0)
    sc[0].emit_pair(0)
    sc[0].send(3, 0)
    for r in (2, 1, 3):
        sc[0].send(r, 1)
    loads[0].wait()
    pool(2, go, st1)
    sc[1].emit_pair(2)
    pool(1, go, st1)
    sc[1].emit_pair(1)
    half = cells // 2

    def pooled_half(q):
        total = sc[0].finish(q)
        wide[q * half:(q + 1) * half] = total
        at = pl.multiple_of(own + q * half, half)
        ext[pl.ds(at, half), :] = total.astype(BF16)
        ag0.start(q)

    pooled_half(0)
    for r in (3, 0):
        pool(r, go, st1)
        sc[1].emit_pair(r)
    pooled_half(1)
    turned[0:feat, :] = jnp.concatenate(
        [jnp.transpose(wide[0:cells].astype(BF16))] * K, axis=1)

    for load in loads[1:]:
        load.wait()
    at_es = pl.multiple_of(f * (edges // L), edges // L)

    @pl.loop(0, edges // L)
    def _(b):
        es_col[pl.ds(pl.multiple_of(b * L, L), L), :] = columns(es[pl.ds(at_es + b, 1), :])

    lane = lax.broadcasted_iota(I32, (L, L), 1)
    sub = lax.broadcasted_iota(I32, (L, L), 0)
    for q in range(2):
        col = columns(halo[q:q + 1, :])

        @pl.loop(0, group // L)
        def _(j, col=col, q=q):
            halo_mat[q * L:(q + 1) * L, pl.ds(pl.multiple_of(j * L, L), L)] = onehot(
                col == lane + j * L)

    for k in range(K):
        for q in range(cells // L):
            at = k * cells + q * L
            col = es_col[pl.ds(k + q * L * K, L, stride=K), :]
            es_row[at // L:at // L + 1, :] = jnp.transpose(col)[0:1, :]

            @pl.loop(0, rows // L)
            def _(j, col=col, at=at):
                src_mat[at:at + L, pl.ds(pl.multiple_of(j * L, L), L)] = onehot(col == lane + j * L)

    for r in (1, 3, 2):
        ag0.share(r, 0)
    for r in (1, 3, 2):
        ag0.share(r, 1)
    for r in (2, 1, 3):
        sc[1].send(r)

    ag0.wait(0, 4, 6, 5)

    def halo_out(q):
        to, row = (right, 0) if q == 0 else (left, side)
        at = group + row
        return pltpu.make_async_remote_copy(
            src_ref=hsend.at[0, q], dst_ref=ext.at[at:at + side, :],
            send_sem=hs_s.at[q], recv_sem=hs_r.at[q],
            device_id={"coarse": to}, device_id_type=MESH)

    picked = dot(halo_mat[...], ext[0:group, :])
    hsend[0, 0] = picked[0:side].astype(BF16)
    hsend[0, 1] = picked[side:2 * side].astype(BF16)
    halo_out(0).start()
    halo_out(1).start()

    acc[0:edges, :] = dot(src_mat[:, 0:group], ext[0:group, :])

    @pl.loop(0, rows // L)
    def _(j):
        at = pl.multiple_of(j * L, L)
        for b in range(edges // L):
            src_mat_t[pl.ds(at, L), b * L:(b + 1) * L] = onehot(es_row[b:b + 1, :] == sub + j * L)

    pooled_bf = wide[0:cells].astype(BF16)
    bias_row = jnp.concatenate([b1[q:q + 1, :].astype(F32) for q in range(n_bias)], axis=1)
    pre_dst = dot(pooled_bf, w1[0:feat, :]) + bias_row
    halo_out(0).wait_recv()
    halo_out(1).wait_recv()
    src_feats = (
        acc[0:edges, :] + dot(src_mat[:, group:rows], ext[group:rows, :])
    ).astype(BF16)
    acc[0:edges, :] = dot(src_feats, w1[feat:2 * feat, :])
    turned[feat:, :] = jnp.transpose(src_feats)

    spans = [slice(k * cells, (k + 1) * cells) for k in range(K)]
    new_coarse = wide[0:cells]
    for span in spans:
        pre = pre_dst + acc[span, :]
        sig = 1.0 / (1.0 + jnp.exp(-pre))
        hidden = (pre * sig).astype(BF16)
        hid[span, :] = hidden
        slope[span, :] = sig * (1.0 + pre * (1.0 - sig))
        new_coarse = new_coarse + dot(hidden, w2[...])
    new_coarse = new_coarse.astype(BF16)

    def spread(r):
        st2[r] = dot(src_mat_t[pl.ds(pair_rows(r), 2 * cells), :], gret[...])
        sc[2].emit_pair(r)

    last = ((1,), (1,))
    gsum = sc[1].finish().astype(BF16)
    gnew = dot(gsum, w3[...], last).astype(BF16)
    ghid = dot(gnew, w2[...], last)
    act_sum = jnp.zeros((cells, feat), F32)
    for span in spans:
        act = (ghid * slope[span, :]).astype(BF16)
        gret[span, :] = act
        act_sum = act_sum + act.astype(F32)


    def halo_back(q):
        to = left if q == 0 else right
        return pltpu.make_async_remote_copy(
            src_ref=hsend.at[1, q], dst_ref=back.at[pl.ds(q * side, side), :],
            send_sem=hs_s.at[2 + q], recv_sem=hs_r.at[2 + q],
            device_id={"coarse": to}, device_id_type=MESH)

    w_part[0] = dot(turned[...], gret[...])
    gnew_t = jnp.concatenate([jnp.transpose(gnew)] * K, axis=1)
    w_part[1, 0:feat, :] = jnp.transpose(dot(gnew_t, hid[...]))
    w_part[1, feat:2 * feat, :] = dot(new_coarse, gsum, ((0,), (0,)))
    b_pair_s[...] = jnp.zeros_like(b_pair_s)
    bias = jnp.sum(act_sum, axis=0, keepdims=True)
    for q in range(n_bias):
        b_pair_s[q:q + 1, :] = bias[:, q * L:(q + 1) * L]

    def remote(src, dst, i, to, sems=(ar_s, ar_r)):
        return pltpu.make_async_remote_copy(
            src_ref=src, dst_ref=dst, send_sem=sems[0].at[i], recv_sem=sems[1].at[i],
            device_id=to, device_id_type=MESH)

    small = (br_s, br_r)
    partner = {"fine": place["partner"]}
    pair_w = remote(w_pair_s, w_pair_r, 0, partner)
    pair_b = remote(b_pair_s, b_pair_r, 0, partner, small)
    w_pair_s[...] = w_part[1 - core].astype(BF16)
    pair_w.start()
    pair_b.start()

    spread(2)
    spread(1)

    piece = 2 * feat // n_coarse
    far = sorted(range(nz), key=lambda d: (-min(d, nz - d), d))
    near = sorted(range(nz), key=lambda d: (min(d, nz - d), d))
    lot = nz // 2
    pair_w.wait_recv()
    for i in range(nx):
        for p in range(nz):
            at = pl.multiple_of((i * nz + lax.rem(z + far[p], nz)) * piece, piece)
            w_rs[i, p] = (
                w_part[core, pl.ds(at, piece), :] + w_pair_r[pl.ds(at, piece), :].astype(F32)
            ).astype(BF16)

    def x_copy(d, h):
        part = pl.ds(h * lot, lot)
        return remote(w_rs.at[lax.rem(x + d, nx), part], w_x.at[d - 1, part],
                      1 + h * (nx - 1) + d - 1, {"coarse": x_peer[d]})

    def z_copy(p):
        return remote(w_z_s.at[p], w_z_r.at[p], 7 + p, {"coarse": z_peer[far[p]]})

    def bx_copy(d, at):
        return remote(b_x.at[at], b_x.at[at], d, {"coarse": x_peer[d]}, small)

    def bz_copy(d, at):
        return remote(b_z.at[at], b_z.at[at], 3 + d, {"coarse": z_peer[d]}, small)

    def by_copy(t, at):
        return remote(b_y.at[at], b_y.at[at], 10 + t, {"fine": place["step"][t]}, small)

    for h in range(2):
        for d in range(1, nx):
            x_copy(d, h).start()
    outer = dot(src_mat_t[group:rows, :], gret[...])
    hsend[1, 0] = outer[0:side].astype(BF16)
    hsend[1, 1] = outer[side:2 * side].astype(BF16)
    halo_back(0).start()
    halo_back(1).start()
    pair_b.wait_recv()
    b_x[x] = b_pair_s[...] + b_pair_r[...]
    for d in range(1, nx):
        bx_copy(d, x).start()

    spread(3)
    spread(0)
    for q in range(2):
        for r in (2, 1, 3):
            sc[2].send(r, q)

    for h in range(2):
        for d in range(1, nx):
            x_copy(d, h).wait_recv()
        for p in range(h * lot, (h + 1) * lot):
            total = w_rs[x, p].astype(F32)
            for d in range(1, nx):
                total = total + w_x[d - 1, p].astype(F32)
            if p < nz - 1:
                w_z_s[p] = total.astype(BF16)
                z_copy(p).start()
            else:
                w_own[...] = total
    for d in range(1, nx):
        bx_copy(d, lax.rem(x + nx - d, nx)).wait_recv()
    total = b_x[0]
    for i in range(1, nx):
        total = total + b_x[i]
    b_z[z] = total
    for d in range(1, nz):
        bz_copy(d, z).start()

    halo_back(0).wait_recv()
    halo_back(1).wait_recv()
    for r in (2, 1, 3, 0):
        at = pl.multiple_of(y_of[r] * 2 * share, 2 * share)
        st3[r] = back[pl.ds(at, 2 * share), :].astype(F32)
        sc[3].emit_pair(r)

    @pl.loop(0, nodes // L)
    def _(b):
        col = columns(cid[pl.ds(b, 1), :])
        at = pl.multiple_of(b * L, L)
        for j in range(group // L):
            unpool_mat[pl.ds(at, L), j * L:(j + 1) * L] = onehot(
                col == lane + (g * group + j * L))
        for q in range(2):
            list_mat[pl.ds(at, L), q * L:(q + 1) * L] = onehot(
                col == halo[q:q + 1, :] + g * group)

    for r in (2, 1, 3):
        sc[3].send(r)
    gpool = gnew.astype(F32)
    for k in range(K):
        gpool = gpool + dot(gret[k * cells:(k + 1) * cells, :], w1[0:feat, :], last)

    total = w_own[...]
    for p in range(nz - 1):
        z_copy(p).wait_recv()
        total = total + w_z_r[p].astype(F32)
    w_y[y] = total

    def y_copy(t, at):
        return remote(w_y.at[at], w_y.at[at], 14 + t, {"fine": place["step"][t]})

    for t in (2, 1, 3):
        y_copy(t, y).start()
    for d in range(1, nz):
        bz_copy(d, lax.rem(z + nz - d, nz)).wait_recv()
    total = b_z[0]
    for i in range(1, nz):
        total = total + b_z[i]
    b_y[y] = total
    for t in (2, 1, 3):
        by_copy(t, y).start()

    for q in range(2):
        src_grad = dot(sc[2].finish(q).astype(BF16), w1[feat:, :], last)
        at = pl.multiple_of(own + q * half, half)
        gp[pl.ds(at, half), :] = (gpool[q * half:(q + 1) * half] + src_grad).astype(BF16)
        ag1.start(q)
    returned = dot(sc[3].finish().astype(BF16), w1[feat:, :], last)
    hb[pl.ds(pl.multiple_of(f * share, share), share), :] = returned.astype(BF16)
    ag2.start()

    def take(y_at, first_pass):
        at = pl.multiple_of(y_at * 2 * cells, 2 * cells)
        part = dot(unpool_mat[:, pl.ds(at, 2 * cells)], gp[pl.ds(at, 2 * cells), :])
        if first_pass:
            acc[...] = part
        else:
            acc[...] += part

    for t in (1, 2, 3):
        y_copy(t, y_of[NY - t]).wait_recv()
    summed = w_y[0]
    for t in range(1, NY):
        summed = summed + w_y[t]
    w_ag[x, 0] = summed.astype(BF16)

    def z_back(d):
        return remote(w_ag.at[x, 0], w_ag.at[x, near.index((nz - d) % nz)],
                      17 + near.index((nz - d) % nz), {"coarse": z_peer[d]})

    def z_here(q):
        ref = w_ag.at[x, q]
        return remote(ref, ref, 17 + q, {"coarse": z_peer[1]})

    def x_back(d, h, at):
        ref = w_ag.at[at, pl.ds(h * lot, lot)]
        return remote(ref, ref, 25 + h * (nx - 1) + d - 1, {"coarse": x_peer[d]})

    for d in far[:-1]:
        z_back(d).start()
    ag1.wait(0)
    take(y, True)

    def forward(h):
        for q in range(max(1, h * lot), (h + 1) * lot):
            z_here(q).wait_recv()
        for d in range(1, nx):
            x_back(d, h, x).start()

    forward(0)
    for q in range(2):
        for r in (1, 3, 2):
            ag1.share(r, q)
    for r in (1, 3, 2):
        ag2.share(r)
    forward(1)
    ag1.wait(4)
    take(y_of[3], False)
    ag1.wait(6)
    take(y_of[1], False)
    ag2.wait(0, 4, 6, 5)
    acc[...] += dot(list_mat[...], hb[...])
    ag1.wait(5)
    at_far = pair_rows(2)

    @pl.loop(0, nodes // (2 * cells))
    def _(b):
        at = pl.ds(pl.multiple_of(b * 2 * cells, 2 * cells), 2 * cells)
        part = dot(unpool_mat[at, pl.ds(at_far, 2 * cells)], gp[pl.ds(at_far, 2 * cells), :])
        out_gf[at, :] = (go[at, :].astype(F32) + (acc[at, :] + part)).astype(BF16)

    for h in range(2):
        for d in range(1, nx):
            x_back(d, h, lax.rem(x + nx - d, nx)).wait_recv()
    pair_fin = remote(w_ag, w_fin.at[core], 31, partner)
    pair_fin.start()
    w_fin[core] = w_ag[...]
    for t in (1, 2, 3):
        by_copy(t, y_of[NY - t]).wait_recv()
    total = b_y[0]
    for t in range(1, NY):
        total = total + b_y[t]
    for q in range(n_bias):
        out_b1[:, q * L:(q + 1) * L] = total[q:q + 1, :] * edge_scale

    def emit(h):
        for i in range(nx):
            for q in range(nz):
                at = lax.rem(z + near[q], nz) * piece
                value = w_fin[h, i, q].astype(F32)
                if h == 0:
                    here = pl.ds(pl.multiple_of(i * nz * piece + at, piece), piece)
                    out_w1[here, :] = value * edge_scale
                elif i < nx // 2:
                    here = pl.ds(pl.multiple_of(i * nz * piece + at, piece), piece)
                    out_w2[here, :] = value * edge_scale
                else:
                    here = pl.ds(pl.multiple_of((i - nx // 2) * nz * piece + at, piece), piece)
                    out_w3[here, :] = value * cell_scale

    @pl.when(core == 0)
    def _():
        emit(0)

    @pl.when(core == 1)
    def _():
        emit(1)

    for s in sc:
        s.drain()
    ag0.drain()
    ag1.drain()
    ag2.drain()
    for q in range(2):
        halo_out(q).wait_send()
        halo_back(q).wait_send()
    pair_w.wait_send()
    pair_b.wait_send()
    for h in range(2):
        for d in range(1, nx):
            x_copy(d, h).wait_send()
            x_back(d, h, x).wait_send()
    for d in range(1, nx):
        bx_copy(d, x).wait_send()
    for p in range(nz - 1):
        z_copy(p).wait_send()
    for d in range(1, nz):
        bz_copy(d, z).wait_send()
        z_back(d).wait_send()
    for t in (1, 2, 3):
        y_copy(t, y).wait_send()
        by_copy(t, y).wait_send()
    pair_fin.wait_send()
    remote(w_ag, w_fin.at[1 - core], 31, partner).wait_recv()

    @pl.when(core == 0)
    def _():
        emit(1)

    @pl.when(core == 1)
    def _():
        emit(0)


def store(*refs):
    count = (len(refs) - 1) // 2
    copies = [
        pltpu.make_async_copy(refs[i], refs[count + i], refs[-1].at[i]) for i in range(count)
    ]
    for copy in copies:
        copy.start()
    for copy in copies:
        copy.wait()


def local(
    node_feats, grad_out, cluster_ids, halo_lists, edge_sources,
    w_edge_in, b_edge_in, w_edge_out, w_unpool,
):
    nodes, feat = node_feats.shape
    group = edge_sources.shape[0] // K
    cells = group // 8
    edges = K * cells
    side = halo_lists.shape[0] // 2
    rows = group + 2 * side
    n_coarse = lax.axis_size("coarse")
    edge_scale = float(group * n_coarse * K) ** -0.5
    cell_scale = float(group * n_coarse) ** -0.5
    share = 2 * side // 8
    piece = 2 * feat // n_coarse
    nx = 4 if n_coarse > 4 else 2
    nz = n_coarse // nx
    vmem = pltpu.VMEM
    dma = pltpu.SemaphoreType.DMA
    results = (
        ((nodes, feat), BF16), ((2 * feat, feat), F32), ((1, feat), F32),
        ((feat, feat), F32), ((feat, feat), F32),
    )
    in_vmem = pl.BlockSpec(memory_space=vmem)
    anywhere = pl.BlockSpec(memory_space=pl.ANY)
    parts = pl.pallas_call(
        functools.partial(kernel, n_coarse, nx, edge_scale, cell_scale),
        out_shape=tuple(pltpu.VMEM(shape, kind) for shape, kind in results),
        in_specs=[anywhere] * 9,
        out_specs=(in_vmem,) * 5,
        scratch_shapes=[
            vmem((nodes // L, L), I32),
            vmem((2, side), I32),
            vmem((group * K // L, L), I32),
            vmem((feat // L, L), BF16),
            vmem((nodes, feat), BF16),
            vmem((nodes, feat), BF16),
            vmem((2 * feat, feat), BF16),
            vmem((feat, feat), BF16),
            vmem((feat, feat), BF16),
            vmem((NY, 2 * cells, nodes), BF16),
            vmem((nodes, group), BF16),
            vmem((edges, rows), BF16),
            vmem((rows, edges), BF16),
            vmem((2 * side, group), BF16),
            vmem((nodes, 2 * side), BF16),
            vmem((edges, L), I32),
            vmem((edges // L, L), I32),
            vmem((NY, 2 * cells, feat), F32),
            vmem((NY, 2 * cells, feat), F32),
            vmem((NY, 2 * cells, feat), F32),
            vmem((3, NY, cells, feat), BF16),
            vmem((3, NY, cells, feat), BF16),
            vmem((3, 3, cells, feat), BF16),
            vmem((3, 3, cells, feat), BF16),
            vmem((NY, 2 * share, feat), F32),
            vmem((NY, share, feat), BF16),
            vmem((NY, share, feat), BF16),
            vmem((3, share, feat), BF16),
            vmem((3, share, feat), BF16),
            vmem((2 * side, feat), BF16),
            vmem((rows, feat), BF16),
            vmem((group, feat), BF16),
            vmem((2, 2, side, feat), BF16),
            vmem((edges, feat), BF16),
            vmem((2 * side, feat), BF16),
            vmem((2 * feat, edges), BF16),
            vmem((edges, feat), BF16),
            vmem((edges, feat), F32),
            vmem((2 * cells, feat), F32),
            vmem((nodes, feat), F32),
            vmem((2, 2 * feat, feat), F32),
            vmem((2 * feat, feat), BF16),
            vmem((2 * feat, feat), BF16),
            vmem((nx, nz, piece, feat), BF16),
            vmem((nx - 1, nz, piece, feat), BF16),
            vmem((piece, feat), F32),
            vmem((nz - 1, piece, feat), BF16),
            vmem((nz - 1, piece, feat), BF16),
            vmem((NY, piece, feat), F32),
            vmem((nx, nz, piece, feat), BF16),
            vmem((2, nx, nz, piece, feat), BF16),
            vmem((8, L), F32),
            vmem((8, L), F32),
            vmem((nx, 8, L), F32),
            vmem((nz, 8, L), F32),
            vmem((NY, 8, L), F32),
            dma((12,)),
            dma((4, NY, 2)), dma((4, NY, 2)), dma((4, 3, 2)), dma((4, 3, 2)),
            dma((3, 7, 2)), dma((3, 7, 2)),
            dma((4,)), dma((4,)),
            dma((32,)), dma((32,)),
            dma((14,)), dma((14,)),
        ],
        compiler_params=pltpu.CompilerParams(
            collective_id=0, has_side_effects=True, vmem_limit_bytes=58 * 2**20),
    )(
        cluster_ids.reshape(nodes // L, L),
        halo_lists.reshape(2, side),
        edge_sources.reshape(group * K // L, L),
        b_edge_in.reshape(feat // L, L),
        node_feats, grad_out, w_edge_in, w_edge_out, w_unpool,
    )
    out = pl.pallas_call(
        store,
        out_shape=tuple(jax.ShapeDtypeStruct(shape, kind) for shape, kind in results),
        in_specs=[anywhere] * 5,
        out_specs=(anywhere,) * 5,
        scratch_shapes=[dma((5,))],
        compiler_params=pltpu.CompilerParams(vmem_limit_bytes=2**20),
    )(*[pltpu.with_memory_space_constraint(part, pltpu.VMEM) for part in parts])
    return out[0], out[1], out[2].reshape(feat), out[3], out[4]


def solution(mesh):
    return jax.shard_map(
        local,
        mesh=mesh,
        in_specs=(
            P(("coarse", "fine"), None), P(("coarse", "fine"), None), P(("coarse", "fine")),
            P("coarse"), P("coarse"), P(), P(), P(), P(),
        ),
        out_specs=(P(("coarse", "fine"), None), P(), P(), P(), P()),
        check_vma=False,
    )
```

```python
import functools

import jax
import jax.numpy as jnp
from jax import lax
from jax.experimental import pallas as pl
from jax.experimental.pallas import tpu as pltpu
from jax.sharding import PartitionSpec as P

MESH = pl.DeviceIdType.MESH
F32 = jnp.float32
BF16 = jnp.bfloat16
I32 = jnp.int32
K = 4
NY = 4
L = 128


def dot(a, b, dims=((1,), (0,))):
    return lax.dot_general(a, b, (dims, ((), ())), preferred_element_type=F32)


def onehot(mask):
    return jnp.where(mask, 1.0, 0.0).astype(BF16)


def onehot16(mask):
    return jnp.where(mask, jnp.ones((), BF16), jnp.zeros((), BF16))


def columns(row):
    return jnp.transpose(jnp.broadcast_to(row, (L, L)))


class Scatter:
    def __init__(self, place, stage, psend, prcv, ysend, yrcv, sems, lots=1):
        self.p = place
        self.stage, self.psend, self.prcv = stage, psend, prcv
        self.ysend, self.yrcv = ysend, yrcv
        self.ps, self.pr, self.ys, self.yr = sems
        self.cells = psend.shape[1]
        self.lots, self.rows = lots, psend.shape[1] // lots

    def part(self, q):
        return pl.ds(q * self.rows, self.rows)

    def pair(self, r, q):
        return pltpu.make_async_remote_copy(
            src_ref=self.psend.at[r, self.part(q)], dst_ref=self.prcv.at[r, self.part(q)],
            send_sem=self.ps.at[r, q], recv_sem=self.pr.at[r, q],
            device_id={"fine": self.p["partner"]}, device_id_type=MESH)

    def ring(self, r, q):
        return pltpu.make_async_remote_copy(
            src_ref=self.ysend.at[r - 1, self.part(q)], dst_ref=self.yrcv.at[r - 1, self.part(q)],
            send_sem=self.ys.at[r - 1, q], recv_sem=self.yr.at[r - 1, q],
            device_id={"fine": self.p["step"][r]}, device_id_type=MESH)

    def emit_pair(self, r):
        at = pl.multiple_of((1 - self.p["core"]) * self.cells, self.cells)
        self.psend[r] = self.stage[r, pl.ds(at, self.cells), :].astype(BF16)
        for q in range(self.lots):
            self.pair(r, q).start()

    def chip_sum(self, r, q):
        self.pair(r, q).wait_recv()
        at = pl.multiple_of(self.p["core"] * self.cells + q * self.rows, self.rows)
        return self.stage[r, pl.ds(at, self.rows), :] + self.prcv[r, self.part(q)].astype(F32)

    def send(self, r, q=0):
        self.ysend[r - 1, self.part(q)] = self.chip_sum(r, q).astype(BF16)
        self.ring(r, q).start()

    def finish(self, q=0):
        total = self.chip_sum(0, q)
        for r in (1, 3, 2):
            self.ring(r, q).wait_recv()
            total = total + self.yrcv[r - 1, self.part(q)].astype(F32)
        return total

    def drain(self):
        for q in range(self.lots):
            for r in range(NY):
                self.pair(r, q).wait_send()
            for r in (1, 2, 3):
                self.ring(r, q).wait_send()


class Gather:
    def __init__(self, place, table, cells, sems, lots=1):
        self.p, self.table, self.cells = place, table, cells
        self.lots, self.rows = lots, cells // lots
        self.ss, self.rs = sems

    def copy(self, i, q, to, y, core):
        at = pl.multiple_of((y * 2 + core) * self.cells + q * self.rows, self.rows)
        ref = self.table.at[pl.ds(at, self.rows), :]
        return pltpu.make_async_remote_copy(
            src_ref=ref, dst_ref=ref, send_sem=self.ss.at[i, q], recv_sem=self.rs.at[i, q],
            device_id={"fine": to}, device_id_type=MESH)

    def out(self, i, q):
        p, c = self.p, self.p["core"]
        if i < NY:
            return self.copy(i, q, p["step"][i] if i else p["partner"], p["ys"][0], c)
        return self.copy(i, q, p["partner"], p["ys"][(NY - (i - 3)) % NY], c)

    def arrival(self, i, q):
        p, c = self.p, self.p["core"]
        if i == 0:
            return self.copy(i, q, p["partner"], p["ys"][0], 1 - c)
        if i < NY:
            return self.copy(i, q, p["partner"], p["ys"][NY - i], c)
        return self.copy(i, q, p["partner"], p["ys"][(NY - (i - 3)) % NY], 1 - c)

    def start(self, q=0):
        for i in (2, 1, 3, 0):
            self.out(i, q).start()

    def share(self, i, q=0):
        self.arrival(i, q).wait_recv()
        self.out(i + 3, q).start()

    def wait(self, *which):
        for q in range(self.lots):
            for i in which:
                self.arrival(i, q).wait_recv()

    def drain(self):
        for q in range(self.lots):
            for i in range(7):
                self.out(i, q).wait_send()


def kernel(
    n_coarse, nx, edge_scale, cell_scale,
    cid_hbm, halo_hbm, es_hbm, b1_hbm, nf_hbm, go_hbm, w1_hbm, w2_hbm, w3_hbm,
    out_gf, out_w1, out_b1, out_w2, out_w3,
    cid, halo, es, b1, nf, go, w1, w2, w3,
    pool_mat, unpool_mat, src_mat, src_mat_t, halo_mat, list_mat,
    es_col, es_row,
    st0, st1, st2, psend, prcv, ysend, yrcv,
    st3, psend3, prcv3, ysend3, yrcv3, hb,
    ext, gp, hsend, gret, back, turned, hid, slope, wide, acc,
    w_part, w_pair_s, w_pair_r, w_rs, w_x, w_own, w_z_s, w_z_r, w_y, w_ag, w_fin,
    b_pair_s, b_pair_r, b_x, b_z, b_y,
    ins, ps, pr, ys, yr, ags, agr, hs_s, hs_r, ar_s, ar_r, br_s, br_r,
):
    cells = gp.shape[0] // 8
    group = 8 * cells
    nodes, feat = nf.shape
    edges = K * cells
    side = halo.shape[1]
    rows = group + 2 * side
    n_bias = feat // L
    g = lax.axis_index("coarse")
    f = lax.axis_index("fine")
    core = lax.rem(f, 2)
    y = lax.div(f, 2)
    y_of = tuple(lax.rem(y + r, NY) for r in range(NY))
    place = {
        "core": core, "ys": y_of, "partner": f + 1 - 2 * core,
        "step": tuple(y_r * 2 + core for y_r in y_of),
    }
    right, left = lax.rem(g + 1, n_coarse), lax.rem(g + n_coarse - 1, n_coarse)

    nz = n_coarse // nx
    z, x = lax.div(g, nx), lax.rem(g, nx)
    x_peer = [z * nx + lax.rem(x + d, nx) for d in range(nx)]
    z_peer = [lax.rem(z + d, nz) * nx + x for d in range(nz)]

    quarter = nodes // 4
    first_loads = [pltpu.make_async_copy(cid_hbm, cid, ins.at[4])] + [
        pltpu.make_async_copy(
            nf_hbm.at[pl.ds(i * quarter, quarter), :], nf.at[pl.ds(i * quarter, quarter), :],
            ins.at[5 + i])
        for i in range(4)
    ]
    for load in first_loads:
        load.start()
    barrier = pltpu.get_barrier_semaphore()
    fine_peers = (place["partner"],) + place["step"][1:]
    coarse_peers = [right, left] + x_peer[1:] + z_peer[1:]
    for to in fine_peers:
        pl.semaphore_signal(barrier, inc=1, device_id={"fine": to}, device_id_type=MESH)
    for to in coarse_peers:
        pl.semaphore_signal(barrier, inc=1, device_id={"coarse": to}, device_id_type=MESH)
    loads = [
        pltpu.make_async_copy(a, b, ins.at[i])
        for i, (a, b) in enumerate(
            ((go_hbm, go), (w1_hbm, w1), (w2_hbm, w2), (w3_hbm, w3)))
    ] + [
        pltpu.make_async_copy(a, b, ins.at[9 + i])
        for i, (a, b) in enumerate(((halo_hbm, halo), (es_hbm, es), (b1_hbm, b1)))
    ]
    for load in loads:
        load.start()

    own = pl.multiple_of(f * cells, cells)

    def pair_rows(r):
        return pl.multiple_of(y_of[r] * 2 * cells, 2 * cells)

    cell_ids = lax.broadcasted_iota(I32, (2 * cells, L), 0).astype(jnp.int16)

    def build_pool(r):
        base = g * group + y_of[r] * 2 * cells
        for b in range(nodes // L):
            row = jnp.broadcast_to(cid[b:b + 1, :] - base, (16, L)).astype(jnp.int16)
            pool_mat[r, :, b * L:(b + 1) * L] = onehot16(
                cell_ids == jnp.concatenate([row] * (2 * cells // 16), axis=0))

    sc = [
        Scatter(place, st, psend.at[i], prcv.at[i], ysend.at[i], yrcv.at[i],
                (ps.at[i], pr.at[i], ys.at[i], yr.at[i]), 1 if i == 1 else 2)
        for i, st in enumerate((st0, st1, st2))
    ]
    sc.append(Scatter(place, st3, psend3, prcv3, ysend3, yrcv3,
                      (ps.at[3], pr.at[3], ys.at[3], yr.at[3])))
    ag0 = Gather(place, ext, cells, (ags.at[0], agr.at[0]), 2)
    ag1 = Gather(place, gp, cells, (ags.at[1], agr.at[1]), 2)
    share = hb.shape[0] // 8
    ag2 = Gather(place, hb, share, (ags.at[2], agr.at[2]))

    def pool(r, x, stage):
        stage[r] = dot(pool_mat[r], x[...])

    first_loads[0].wait()
    build_pool(2)
    for load in first_loads[1:]:
        load.wait()
    pool(2, nf, st0)
    pl.semaphore_wait(barrier, len(fine_peers) + len(coarse_peers))
    sc[0].emit_pair(2)
    build_pool(1)
    pool(1, nf, st0)
    sc[0].emit_pair(1)
    sc[0].send(2, 0)
    build_pool(3)
    pool(3, nf, st0)
    sc[0].emit_pair(3)
    sc[0].send(1, 0)
    build_pool(0)
    pool(0, nf, st0)
    sc[0].emit_pair(0)
    sc[0].send(3, 0)
    for r in (2, 1, 3):
        sc[0].send(r, 1)
    loads[0].wait()
    pool(2, go, st1)
    sc[1].emit_pair(2)
    pool(1, go, st1)
    sc[1].emit_pair(1)
    half = cells // 2

    def pooled_half(q):
        total = sc[0].finish(q)
        wide[q * half:(q + 1) * half] = total
        at = pl.multiple_of(own + q * half, half)
        ext[pl.ds(at, half), :] = total.astype(BF16)
        ag0.start(q)

    pooled_half(0)
    for r in (3, 0):
        pool(r, go, st1)
        sc[1].emit_pair(r)
    pooled_half(1)
    turned[0:feat, :] = jnp.concatenate(
        [jnp.transpose(wide[0:cells].astype(BF16))] * K, axis=1)

    for load in loads[1:]:
        load.wait()
    at_es = pl.multiple_of(f * (edges // L), edges // L)

    @pl.loop(0, edges // L)
    def _(b):
        es_col[pl.ds(pl.multiple_of(b * L, L), L), :] = columns(es[pl.ds(at_es + b, 1), :])

    lane = lax.broadcasted_iota(I32, (L, L), 1)
    sub = lax.broadcasted_iota(I32, (L, L), 0)
    for q in range(2):
        col = columns(halo[q:q + 1, :])

        @pl.loop(0, group // L)
        def _(j, col=col, q=q):
            halo_mat[q * L:(q + 1) * L, pl.ds(pl.multiple_of(j * L, L), L)] = onehot(
                col == lane + j * L)

    for k in range(K):
        for q in range(cells // L):
            at = k * cells + q * L
            col = es_col[pl.ds(k + q * L * K, L, stride=K), :]
            es_row[at // L:at // L + 1, :] = jnp.transpose(col)[0:1, :]

            @pl.loop(0, rows // L)
            def _(j, col=col, at=at):
                src_mat[at:at + L, pl.ds(pl.multiple_of(j * L, L), L)] = onehot(col == lane + j * L)

    for r in (1, 3, 2):
        ag0.share(r, 0)
    for r in (1, 3, 2):
        ag0.share(r, 1)
    for r in (2, 1, 3):
        sc[1].send(r)

    ag0.wait(0, 4, 6, 5)

    def halo_out(q):
        to, row = (right, 0) if q == 0 else (left, side)
        at = group + row
        return pltpu.make_async_remote_copy(
            src_ref=hsend.at[0, q], dst_ref=ext.at[at:at + side, :],
            send_sem=hs_s.at[q], recv_sem=hs_r.at[q],
            device_id={"coarse": to}, device_id_type=MESH)

    picked = dot(halo_mat[...], ext[0:group, :])
    hsend[0, 0] = picked[0:side].astype(BF16)
    hsend[0, 1] = picked[side:2 * side].astype(BF16)
    halo_out(0).start()
    halo_out(1).start()

    acc[0:edges, :] = dot(src_mat[:, 0:group], ext[0:group, :])

    @pl.loop(0, rows // L)
    def _(j):
        at = pl.multiple_of(j * L, L)
        for b in range(edges // L):
            src_mat_t[pl.ds(at, L), b * L:(b + 1) * L] = onehot(es_row[b:b + 1, :] == sub + j * L)

    pooled_bf = wide[0:cells].astype(BF16)
    bias_row = jnp.concatenate([b1[q:q + 1, :].astype(F32) for q in range(n_bias)], axis=1)
    pre_dst = dot(pooled_bf, w1[0:feat, :]) + bias_row
    halo_out(0).wait_recv()
    halo_out(1).wait_recv()
    src_feats = (
        acc[0:edges, :] + dot(src_mat[:, group:rows], ext[group:rows, :])
    ).astype(BF16)
    acc[0:edges, :] = dot(src_feats, w1[feat:2 * feat, :])
    turned[feat:, :] = jnp.transpose(src_feats)

    spans = [slice(k * cells, (k + 1) * cells) for k in range(K)]
    new_coarse = wide[0:cells]
    for span in spans:
        pre = pre_dst + acc[span, :]
        sig = 1.0 / (1.0 + jnp.exp(-pre))
        hidden = (pre * sig).astype(BF16)
        hid[span, :] = hidden
        slope[span, :] = sig * (1.0 + pre * (1.0 - sig))
        new_coarse = new_coarse + dot(hidden, w2[...])
    new_coarse = new_coarse.astype(BF16)

    def spread(r):
        st2[r] = dot(src_mat_t[pl.ds(pair_rows(r), 2 * cells), :], gret[...])
        sc[2].emit_pair(r)

    last = ((1,), (1,))
    gsum = sc[1].finish().astype(BF16)
    gnew = dot(gsum, w3[...], last).astype(BF16)
    ghid = dot(gnew, w2[...], last)
    act_sum = jnp.zeros((cells, feat), F32)
    for span in spans:
        act = (ghid * slope[span, :]).astype(BF16)
        gret[span, :] = act
        act_sum = act_sum + act.astype(F32)


    def halo_back(q):
        to = left if q == 0 else right
        return pltpu.make_async_remote_copy(
            src_ref=hsend.at[1, q], dst_ref=back.at[pl.ds(q * side, side), :],
            send_sem=hs_s.at[2 + q], recv_sem=hs_r.at[2 + q],
            device_id={"coarse": to}, device_id_type=MESH)

    outer = dot(src_mat_t[group:rows, :], gret[...])
    hsend[1, 0] = outer[0:side].astype(BF16)
    hsend[1, 1] = outer[side:2 * side].astype(BF16)
    halo_back(0).start()
    halo_back(1).start()
    w_part[0] = dot(turned[...], gret[...])
    gnew_t = jnp.concatenate([jnp.transpose(gnew)] * K, axis=1)
    w_part[1, 0:feat, :] = jnp.transpose(dot(gnew_t, hid[...]))
    w_part[1, feat:2 * feat, :] = dot(new_coarse, gsum, ((0,), (0,)))
    b_pair_s[...] = jnp.zeros_like(b_pair_s)
    bias = jnp.sum(act_sum, axis=0, keepdims=True)
    for q in range(n_bias):
        b_pair_s[q:q + 1, :] = bias[:, q * L:(q + 1) * L]

    def remote(src, dst, i, to, sems=(ar_s, ar_r)):
        return pltpu.make_async_remote_copy(
            src_ref=src, dst_ref=dst, send_sem=sems[0].at[i], recv_sem=sems[1].at[i],
            device_id=to, device_id_type=MESH)

    small = (br_s, br_r)
    partner = {"fine": place["partner"]}
    pair_w = remote(w_pair_s, w_pair_r, 0, partner)
    pair_b = remote(b_pair_s, b_pair_r, 0, partner, small)
    w_pair_s[...] = w_part[1 - core].astype(BF16)
    pair_w.start()
    pair_b.start()

    spread(2)
    spread(1)

    piece = 2 * feat // n_coarse
    far = sorted(range(nz), key=lambda d: (-min(d, nz - d), d))
    near = sorted(range(nz), key=lambda d: (min(d, nz - d), d))
    lot = nz // 2
    pair_w.wait_recv()
    def x_copy(d, h):
        part = pl.ds(h * lot, lot)
        return remote(w_rs.at[lax.rem(x + d, nx), part], w_x.at[d - 1, part],
                      1 + h * (nx - 1) + d - 1, {"coarse": x_peer[d]})

    def z_copy(p):
        return remote(w_z_s.at[p], w_z_r.at[p], 7 + p, {"coarse": z_peer[far[p]]})

    def bx_copy(d, at):
        return remote(b_x.at[at], b_x.at[at], d, {"coarse": x_peer[d]}, small)

    def bz_copy(d, at):
        return remote(b_z.at[at], b_z.at[at], 3 + d, {"coarse": z_peer[d]}, small)

    def by_copy(t, at):
        return remote(b_y.at[at], b_y.at[at], 10 + t, {"fine": place["step"][t]}, small)

    for h in range(2):
        for i in range(nx):
            for p in range(h * lot, (h + 1) * lot):
                at = pl.multiple_of((i * nz + lax.rem(z + far[p], nz)) * piece, piece)
                w_rs[i, p] = (
                    w_part[core, pl.ds(at, piece), :] + w_pair_r[pl.ds(at, piece), :].astype(F32)
                ).astype(BF16)
        for d in range(1, nx):
            x_copy(d, h).start()
    pair_b.wait_recv()
    b_x[x] = b_pair_s[...] + b_pair_r[...]
    for d in range(1, nx):
        bx_copy(d, x).start()

    spread(3)
    spread(0)
    for q in range(2):
        for r in (2, 1, 3):
            sc[2].send(r, q)

    for h in range(2):
        for d in range(1, nx):
            x_copy(d, h).wait_recv()
        for p in range(h * lot, (h + 1) * lot):
            total = w_rs[x, p].astype(F32)
            for d in range(1, nx):
                total = total + w_x[d - 1, p].astype(F32)
            if p < nz - 1:
                w_z_s[p] = total.astype(BF16)
                z_copy(p).start()
            else:
                w_own[...] = total
    for d in range(1, nx):
        bx_copy(d, lax.rem(x + nx - d, nx)).wait_recv()
    total = b_x[0]
    for i in range(1, nx):
        total = total + b_x[i]
    b_z[z] = total
    for d in range(1, nz):
        bz_copy(d, z).start()

    halo_back(0).wait_recv()
    halo_back(1).wait_recv()
    for r in (2, 1, 3, 0):
        at = pl.multiple_of(y_of[r] * 2 * share, 2 * share)
        st3[r] = back[pl.ds(at, 2 * share), :].astype(F32)
        sc[3].emit_pair(r)

    @pl.loop(0, nodes // L)
    def _(b):
        col = columns(cid[pl.ds(b, 1), :])
        at = pl.multiple_of(b * L, L)
        for j in range(group // L):
            unpool_mat[pl.ds(at, L), j * L:(j + 1) * L] = onehot(
                col == lane + (g * group + j * L))
        for q in range(2):
            list_mat[pl.ds(at, L), q * L:(q + 1) * L] = onehot(
                col == halo[q:q + 1, :] + g * group)

    for r in (2, 1, 3):
        sc[3].send(r)
    gpool = gnew.astype(F32)
    for k in range(K):
        gpool = gpool + dot(gret[k * cells:(k + 1) * cells, :], w1[0:feat, :], last)

    total = w_own[...]
    for p in range(nz - 1):
        z_copy(p).wait_recv()
        total = total + w_z_r[p].astype(F32)
    w_y[y] = total

    def y_copy(t, at):
        return remote(w_y.at[at], w_y.at[at], 14 + t, {"fine": place["step"][t]})

    for t in (2, 1, 3):
        y_copy(t, y).start()
    for d in range(1, nz):
        bz_copy(d, lax.rem(z + nz - d, nz)).wait_recv()
    total = b_z[0]
    for i in range(1, nz):
        total = total + b_z[i]
    b_y[y] = total
    for t in (2, 1, 3):
        by_copy(t, y).start()

    for q in range(2):
        src_grad = dot(sc[2].finish(q).astype(BF16), w1[feat:, :], last)
        at = pl.multiple_of(own + q * half, half)
        gp[pl.ds(at, half), :] = (gpool[q * half:(q + 1) * half] + src_grad).astype(BF16)
        ag1.start(q)
    returned = dot(sc[3].finish().astype(BF16), w1[feat:, :], last)
    hb[pl.ds(pl.multiple_of(f * share, share), share), :] = returned.astype(BF16)
    ag2.start()

    def take(y_at, core_at):
        at = pl.multiple_of((y_at * 2 + core_at) * cells, cells)
        return dot(unpool_mat[:, pl.ds(at, cells)], gp[pl.ds(at, cells), :])

    for t in (1, 2, 3):
        y_copy(t, y_of[NY - t]).wait_recv()
    summed = w_y[0]
    for t in range(1, NY):
        summed = summed + w_y[t]
    w_ag[x, 0] = summed.astype(BF16)

    def z_back(d):
        return remote(w_ag.at[x, 0], w_ag.at[x, near.index((nz - d) % nz)],
                      17 + near.index((nz - d) % nz), {"coarse": z_peer[d]})

    def z_here(q):
        ref = w_ag.at[x, q]
        return remote(ref, ref, 17 + q, {"coarse": z_peer[1]})

    def x_back(d, h, at):
        ref = w_ag.at[at, pl.ds(h * lot, lot)]
        return remote(ref, ref, 25 + h * (nx - 1) + d - 1, {"coarse": x_peer[d]})

    for d in far[:-1]:
        z_back(d).start()
    acc[...] = take(y, core)
    ag1.wait(0)
    acc[...] += take(y, 1 - core)

    def forward(h):
        for q in range(max(1, h * lot), (h + 1) * lot):
            z_here(q).wait_recv()
        for d in range(1, nx):
            x_back(d, h, x).start()

    forward(0)
    for r in (1, 3, 2):
        ag1.share(r, 0)
    forward(1)
    for r in (1, 3):
        ag1.share(r, 1)
        acc[...] += take(y_of[NY - r], core)
        ag2.share(r)
    ag1.share(2, 1)
    ag2.share(2)
    acc[...] += take(y_of[2], core)
    ag1.wait(4)
    acc[...] += take(y_of[3], 1 - core)
    ag1.wait(6)
    acc[...] += take(y_of[1], 1 - core)
    ag2.wait(0, 4, 6, 5)
    acc[...] += dot(list_mat[...], hb[...])
    ag1.wait(5)
    at_far = pl.multiple_of((y_of[2] * 2 + 1 - core) * cells, cells)

    @pl.loop(0, nodes // (2 * cells))
    def _(b):
        at = pl.ds(pl.multiple_of(b * 2 * cells, 2 * cells), 2 * cells)
        part = dot(unpool_mat[at, pl.ds(at_far, cells)], gp[pl.ds(at_far, cells), :])
        out_gf[at, :] = (go[at, :].astype(F32) + (acc[at, :] + part)).astype(BF16)

    for h in range(2):
        for d in range(1, nx):
            x_back(d, h, lax.rem(x + nx - d, nx)).wait_recv()
    pair_fin = remote(w_ag, w_fin.at[core], 31, partner)
    pair_fin.start()
    w_fin[core] = w_ag[...]
    for t in (1, 2, 3):
        by_copy(t, y_of[NY - t]).wait_recv()
    total = b_y[0]
    for t in range(1, NY):
        total = total + b_y[t]
    for q in range(n_bias):
        out_b1[:, q * L:(q + 1) * L] = total[q:q + 1, :] * edge_scale

    def emit(h):
        for i in range(nx):
            for q in range(nz):
                at = lax.rem(z + near[q], nz) * piece
                value = w_fin[h, i, q].astype(F32)
                if h == 0:
                    here = pl.ds(pl.multiple_of(i * nz * piece + at, piece), piece)
                    out_w1[here, :] = value * edge_scale
                elif i < nx // 2:
                    here = pl.ds(pl.multiple_of(i * nz * piece + at, piece), piece)
                    out_w2[here, :] = value * edge_scale
                else:
                    here = pl.ds(pl.multiple_of((i - nx // 2) * nz * piece + at, piece), piece)
                    out_w3[here, :] = value * cell_scale

    @pl.when(core == 0)
    def _():
        emit(0)

    @pl.when(core == 1)
    def _():
        emit(1)

    for s in sc:
        s.drain()
    ag0.drain()
    ag1.drain()
    ag2.drain()
    for q in range(2):
        halo_out(q).wait_send()
        halo_back(q).wait_send()
    pair_w.wait_send()
    pair_b.wait_send()
    for h in range(2):
        for d in range(1, nx):
            x_copy(d, h).wait_send()
            x_back(d, h, x).wait_send()
    for d in range(1, nx):
        bx_copy(d, x).wait_send()
    for p in range(nz - 1):
        z_copy(p).wait_send()
    for d in range(1, nz):
        bz_copy(d, z).wait_send()
        z_back(d).wait_send()
    for t in (1, 2, 3):
        y_copy(t, y).wait_send()
        by_copy(t, y).wait_send()
    pair_fin.wait_send()
    remote(w_ag, w_fin.at[1 - core], 31, partner).wait_recv()

    @pl.when(core == 0)
    def _():
        emit(1)

    @pl.when(core == 1)
    def _():
        emit(0)


def store(*refs):
    count = (len(refs) - 1) // 2
    copies = [
        pltpu.make_async_copy(refs[i], refs[count + i], refs[-1].at[i]) for i in range(count)
    ]
    for copy in copies:
        copy.start()
    for copy in copies:
        copy.wait()


def local(
    node_feats, grad_out, cluster_ids, halo_lists, edge_sources,
    w_edge_in, b_edge_in, w_edge_out, w_unpool,
):
    nodes, feat = node_feats.shape
    group = edge_sources.shape[0] // K
    cells = group // 8
    edges = K * cells
    side = halo_lists.shape[0] // 2
    rows = group + 2 * side
    n_coarse = lax.axis_size("coarse")
    edge_scale = float(group * n_coarse * K) ** -0.5
    cell_scale = float(group * n_coarse) ** -0.5
    share = 2 * side // 8
    piece = 2 * feat // n_coarse
    nx = 4 if n_coarse > 4 else 2
    nz = n_coarse // nx
    vmem = pltpu.VMEM
    dma = pltpu.SemaphoreType.DMA
    results = (
        ((nodes, feat), BF16), ((2 * feat, feat), F32), ((1, feat), F32),
        ((feat, feat), F32), ((feat, feat), F32),
    )
    in_vmem = pl.BlockSpec(memory_space=vmem)
    anywhere = pl.BlockSpec(memory_space=pl.ANY)
    parts = pl.pallas_call(
        functools.partial(kernel, n_coarse, nx, edge_scale, cell_scale),
        out_shape=tuple(pltpu.VMEM(shape, kind) for shape, kind in results),
        in_specs=[anywhere] * 9,
        out_specs=(in_vmem,) * 5,
        scratch_shapes=[
            vmem((nodes // L, L), I32),
            vmem((2, side), I32),
            vmem((group * K // L, L), I32),
            vmem((feat // L, L), BF16),
            vmem((nodes, feat), BF16),
            vmem((nodes, feat), BF16),
            vmem((2 * feat, feat), BF16),
            vmem((feat, feat), BF16),
            vmem((feat, feat), BF16),
            vmem((NY, 2 * cells, nodes), BF16),
            vmem((nodes, group), BF16),
            vmem((edges, rows), BF16),
            vmem((rows, edges), BF16),
            vmem((2 * side, group), BF16),
            vmem((nodes, 2 * side), BF16),
            vmem((edges, L), I32),
            vmem((edges // L, L), I32),
            vmem((NY, 2 * cells, feat), F32),
            vmem((NY, 2 * cells, feat), F32),
            vmem((NY, 2 * cells, feat), F32),
            vmem((3, NY, cells, feat), BF16),
            vmem((3, NY, cells, feat), BF16),
            vmem((3, 3, cells, feat), BF16),
            vmem((3, 3, cells, feat), BF16),
            vmem((NY, 2 * share, feat), F32),
            vmem((NY, share, feat), BF16),
            vmem((NY, share, feat), BF16),
            vmem((3, share, feat), BF16),
            vmem((3, share, feat), BF16),
            vmem((2 * side, feat), BF16),
            vmem((rows, feat), BF16),
            vmem((group, feat), BF16),
            vmem((2, 2, side, feat), BF16),
            vmem((edges, feat), BF16),
            vmem((2 * side, feat), BF16),
            vmem((2 * feat, edges), BF16),
            vmem((edges, feat), BF16),
            vmem((edges, feat), F32),
            vmem((2 * cells, feat), F32),
            vmem((nodes, feat), F32),
            vmem((2, 2 * feat, feat), F32),
            vmem((2 * feat, feat), BF16),
            vmem((2 * feat, feat), BF16),
            vmem((nx, nz, piece, feat), BF16),
            vmem((nx - 1, nz, piece, feat), BF16),
            vmem((piece, feat), F32),
            vmem((nz - 1, piece, feat), BF16),
            vmem((nz - 1, piece, feat), BF16),
            vmem((NY, piece, feat), F32),
            vmem((nx, nz, piece, feat), BF16),
            vmem((2, nx, nz, piece, feat), BF16),
            vmem((8, L), F32),
            vmem((8, L), F32),
            vmem((nx, 8, L), F32),
            vmem((nz, 8, L), F32),
            vmem((NY, 8, L), F32),
            dma((12,)),
            dma((4, NY, 2)), dma((4, NY, 2)), dma((4, 3, 2)), dma((4, 3, 2)),
            dma((3, 7, 2)), dma((3, 7, 2)),
            dma((4,)), dma((4,)),
            dma((32,)), dma((32,)),
            dma((14,)), dma((14,)),
        ],
        compiler_params=pltpu.CompilerParams(
            collective_id=0, has_side_effects=True, vmem_limit_bytes=58 * 2**20),
    )(
        cluster_ids.reshape(nodes // L, L),
        halo_lists.reshape(2, side),
        edge_sources.reshape(group * K // L, L),
        b_edge_in.reshape(feat // L, L),
        node_feats, grad_out, w_edge_in, w_edge_out, w_unpool,
    )
    out = pl.pallas_call(
        store,
        out_shape=tuple(jax.ShapeDtypeStruct(shape, kind) for shape, kind in results),
        in_specs=[anywhere] * 5,
        out_specs=(anywhere,) * 5,
        scratch_shapes=[dma((5,))],
        compiler_params=pltpu.CompilerParams(vmem_limit_bytes=2**20),
    )(*[pltpu.with_memory_space_constraint(part, pltpu.VMEM) for part in parts])
    return out[0], out[1], out[2].reshape(feat), out[3], out[4]


def solution(mesh):
    return jax.shard_map(
        local,
        mesh=mesh,
        in_specs=(
            P(("coarse", "fine"), None), P(("coarse", "fine"), None), P(("coarse", "fine")),
            P("coarse"), P("coarse"), P(), P(), P(), P(),
        ),
        out_specs=(P(("coarse", "fine"), None), P(), P(), P(), P()),
        check_vma=False,
    )
```
